128 devices in a mesh: var: 8 (over y, z_hi), row: 16 (over z_lo, x, core).
Axes of the slice: x: 4, y: 4, z: 4 (z_hi: 2, z_lo: 2; z = z_hi * 2 + z_lo), core: 2. Of those that a mesh axis runs over, the one named last changes fastest.
Arguments:
- frf: float32 [2, 65536, 1024], P(None, 'row', 'var'), may hold values from -0.078125 to 0.078125
- mount_rows: int32 [256, 4], replicated, may hold values from 0 to 65535, as said below
- recv_rows: int32 [512], replicated, may hold values from 0 to 65535
- codes: int32 [32768, 256], P(('var', 'row')), may hold values from 0 to 7
- stiffness: float32 [8, 4], replicated, may hold values from 0.3 to 0.9
- loss: float32 [8, 4], replicated, may hold values from 0.05 to 0.4
- load: float32 [2, 1024], replicated, may hold values from -6 to 6
Outputs:
- response: float32 [2, 32768, 512], P(None, ('var', 'row'))
The draws below stay inside these ranges and needn't reach their ends.
Inputs may be any that keep to these rules, and one draw needn't show every extreme that they name: `mount_rows`: the 1024 rows are distinct and increasing; entry k of the flattened table lies in [k * (65536 / 1024), (k + 1) * (65536 / 1024)).
All inputs are finite; a program needn't handle non-finite values.
Results may differ from the reference program's by a relative error of at most 0.0001.
Values sent between devices are 32-bit elements; how exact they have to be, the bound alone decides.
A program may use at most 128 MiB of HBM per device.

```python
import math
import jax
import jax.numpy as jnp
from jax import lax

C = 1024
R = 512
LEVELS = 8
ITERS = 4
M = 256
NDOF = 65536
VARIANTS = 32768


def draw_mount_rows(key, part):
    stride = NDOF // C
    offsets = jax.random.randint(key, (C,), 0, stride)
    flat = jnp.arange(C, dtype=jnp.int32) * stride + offsets
    return flat.reshape(M, 4).astype(jnp.int32)


def set_ends(drawn, own_key, low, top_value):
    place = [jax.random.randint(jax.random.fold_in(own_key, axis), (), 0, length) for axis, length in enumerate(drawn.shape)]
    longest = drawn.shape.index(max(drawn.shape))
    neighbour = place[:longest] + [(place[longest] + 1) % drawn.shape[longest]] + place[longest + 1:]
    return drawn.at[tuple(place)].set(low).at[tuple(neighbour)].set(top_value)


def shard_levels(rng, extent, split, least, high):
    def one(position, blocks):
        draws = jax.random.uniform(jax.random.fold_in(jax.random.fold_in(rng, 6), position), (blocks,), jnp.float32, least / len(split), high / len(split))
        return jnp.repeat(jnp.exp(draws), extent[position] // blocks).reshape((-1,) + (1,) * (len(extent) - position - 1))

    level = one(*split[0])
    for cut in split[1:]:
        level = level * one(*cut)
    return level


def scatter_about(stream_key, shape, deviation, bound, shards=(), held_as=jnp.bfloat16):
    entries = jax.random.normal(stream_key, shape, jnp.float32) * deviation
    if len(shards) > 0:
        entries = shard_levels(stream_key, shape, shards, -0.22, 0.18) * entries
    return jnp.clip(entries, min=-bound, max=bound).astype(held_as)


def setup_inputs(seed: int = 0) -> dict:
    arg_keys = jax.random.split(jax.random.key(seed), 8)
    return {
        "frf": scatter_about(arg_keys[0], (2, NDOF, C), (6 * C) ** -0.5, 0.078125, ((1, 16), (2, 8)), jnp.float32),
        "mount_rows": draw_mount_rows(jax.random.fold_in(arg_keys[7], 71), 0),
        "recv_rows": set_ends(jax.random.randint(arg_keys[2], (R,), 0, NDOF), jax.random.fold_in(arg_keys[2], 1), 0, NDOF - 1).astype(jnp.int32),
        "codes": set_ends(jax.random.randint(arg_keys[3], (VARIANTS, M), 0, LEVELS), jax.random.fold_in(arg_keys[3], 1), 0, LEVELS - 1).astype(jnp.int32),
        "stiffness": jnp.clip(jnp.exp(jax.random.uniform(arg_keys[4], (LEVELS, 4), jnp.float32, math.log(0.3), math.log(0.9))), 0.3, 0.9),
        "loss": jnp.clip(jax.random.uniform(arg_keys[5], (LEVELS, 4), jnp.float32, 0.05, 0.4), 0.05, 0.4),
        "load": scatter_about(arg_keys[6], (2, C), 1.0, 6.0, (), jnp.float32),
    }


def complex_apply(z_re, z_im, mat_re, mat_im):
    count = z_re.shape[0]
    stacked = jnp.concatenate([z_re, z_im], 0)
    dims = (((1,), (1,)), ((), ()))
    first = lax.dot_general(stacked, mat_re, dims, precision=lax.Precision.HIGHEST, preferred_element_type=jnp.float32)
    second = lax.dot_general(stacked, mat_im, dims, precision=lax.Precision.HIGHEST, preferred_element_type=jnp.float32)
    return first[:count] - second[count:], second[:count] + first[count:]


def lookup(codes, stiffness, loss):
    levels = stiffness.shape[0]
    onehot = (codes[:, :, None] == jnp.arange(levels, dtype=jnp.int32)[None, None, :]).astype(jnp.float32)
    level_k = jnp.einsum("vml,ld->vmd", onehot, stiffness, precision=lax.Precision.HIGHEST)
    level_e = jnp.einsum("vml,ld->vmd", onehot, loss, precision=lax.Precision.HIGHEST)
    delta_re = level_k.reshape(codes.shape[0], -1)
    delta_im = (level_k * level_e).reshape(codes.shape[0], -1)
    return delta_re, delta_im


def series(coupled, receive, delta_re, delta_im, load):
    load_re = jnp.broadcast_to(load[0][None, :], delta_re.shape)
    load_im = jnp.broadcast_to(load[1][None, :], delta_re.shape)
    z_re, z_im = load_re, load_im
    for step in range(ITERS):
        y_re, y_im = complex_apply(z_re, z_im, coupled[0], coupled[1])
        z_re = load_re - (delta_re * y_re - delta_im * y_im)
        z_im = load_im - (delta_re * y_im + delta_im * y_re)
    out_re, out_im = complex_apply(z_re, z_im, receive[0], receive[1])
    return jnp.stack([out_re, out_im], 0)


def reference(frf, mount_rows, recv_rows, codes, stiffness, loss, load):
    conn = mount_rows.reshape(-1).astype(jnp.int32)
    coupled = jnp.take(frf, conn, axis=1)
    receive = jnp.take(frf, recv_rows.astype(jnp.int32), axis=1)
    delta_re, delta_im = lookup(codes, stiffness, loss)
    return series(coupled, receive, delta_re, delta_im, load)
```

```python
import functools

import jax
import jax.numpy as jnp
from jax import lax
from jax.experimental import pallas as pl
from jax.experimental.pallas import tpu as pltpu
from jax.sharding import PartitionSpec as P

MESH = pl.DeviceIdType.MESH
F32, BF16 = jnp.float32, jnp.bfloat16
ITERS = 4
LEVELS = 8
GRANULE = ((0, 0), (0, 1), (0, 2), (1, 0), (1, 1), (1, 2), (2, 0), (2, 1))
PART = (3, 3, 2)
ORDER = (1, 3, 2)
NREC = 20


def device(x, y, z, k):
    return {"var": y * 2 + z // 2, "row": (z % 2) * 8 + x * 2 + k}


class Net:
    def __init__(self):
        v, r = lax.axis_index("var"), lax.axis_index("row")
        y, zh = v // 2, v % 2
        zl, x, k = r // 8, (r // 2) % 4, r % 2
        z = zh * 2 + zl
        self.v, self.r, self.zl, self.zh, self.k = v, r, zl, zh, k
        self.pos = (x, y, z)
        self.near = {}
        for a in range(3):
            for d in (1, 2, 3):
                c = [x, y, z]
                c[a] = (c[a] + d) % 4
                self.near[a, d] = device(*c, k)
        self.sib = device(x, y, z, 1 - k)
        self.pair = {"var": v, "row": (1 - zl) * 8 + x * 2 + k}
        self.same_row = [{"var": (v + i) % 8, "row": r} for i in range(1, 8)]
        self.same_var = [{"var": v, "row": (r + i) % 16} for i in range(1, 16)]

    def along(self, turn, d):
        m, n = self.near[turn % 3, d], self.near[(turn + 1) % 3, d]
        return {q: jnp.where(self.k == 0, m[q], n[q]) for q in ("var", "row")}

    def greet(self):
        sem = pltpu.get_barrier_semaphore()
        for d in list(self.near.values()) + self.same_row + self.same_var:
            pl.semaphore_signal(sem, inc=1, device_id=d, device_id_type=MESH)

    def greeted(self):
        pl.semaphore_wait(pltpu.get_barrier_semaphore(), 9 + 7 + 15)


def slot(k, d3, d2, d1=0, n=1):
    return pl.ds(((k * 4 + d3) * 4 + d2) * 4 + d1, n)


class Gather:
    def __init__(self, group, bufs, send, recv, net, size_ref):
        self.group, self.bufs, self.net, self.size_ref = group, bufs, net, size_ref
        self.send, self.recv = send.at[group], recv
        self.count = 0

    def sem(self, kind, i=0):
        return self.recv.at[self.group * NREC + {"a": 0, "b": 0, "c": 4, "s": 16}[kind] + i]

    def go(self, p, src, dst, sem, dev):
        pltpu.make_async_remote_copy(
            src_ref=self.bufs[p].at[src], dst_ref=self.bufs[p].at[dst], send_sem=self.send, recv_sem=sem,
            device_id=dev, device_id_type=MESH).start()

    def wait(self, n, sem):
        ref = self.size_ref.at[pl.ds(0, n)]
        pltpu.make_async_copy(ref, ref, sem).wait()

    def dev(self, p, axis, d):
        return self.net.along(p + axis - 1 + self.group, d)

    def first(self):
        k = self.net.k
        for p in range(3):
            for d in ORDER:
                self.go(p, slot(k, 0, 0), slot(k, 0, 0, 4 - d), self.sem("a"), self.dev(p, 1, d))
        for p in range(3):
            self.send_b(p, (0, 1))
        for p in range(3):
            self.send_c(p, 0, (0, 1))

    def send_b(self, p, what):
        k = self.net.k
        for d in ORDER:
            self.go(p, slot(k, 0, 0, *what), slot(k, 0, 4 - d, *what), self.sem("b", d), self.dev(p, 2, d))

    def send_c(self, p, d2, what):
        k = self.net.k
        for d in ORDER:
            self.go(p, slot(k, 0, d2, *what), slot(k, 4 - d, d2, *what), self.sem("c", d2 * 3 + d - 1), self.dev(p, 3, d))

    def core(self, d3, d2):
        at = slot(self.net.k, d3, d2, 0, 4)
        for p in range(3):
            self.go(p, at, at, self.sem("s", d3), self.net.sib)

    def second(self):
        self.wait(3, self.sem("a"))
        for p in range(3):
            self.send_b(p, (1, 3))
        for p in range(3):
            self.send_c(p, 0, (1, 3))
        self.core(0, 0)

    def third(self, d):
        self.wait(4, self.sem("b", d))
        for p in range(3):
            self.send_c(p, 4 - d, (0, 4))
        self.core(0, 4 - d)

    def last(self, d2, d):
        self.wait(4, self.sem("c", d2 * 3 + d - 1))
        self.core(4 - d, d2)

    def lasts(self, *lines):
        for d2 in lines:
            for d in ORDER:
                self.last(d2, d)

    def cores(self):
        for d3 in range(4):
            self.wait(16, self.sem("s", d3))

    def end(self, frf_v):
        ref = frf_v.at[:, pl.ds(0, 127 * 32), :]
        pltpu.make_async_copy(ref, ref, self.send).wait()


def halves(x):
    hi = x.astype(BF16)
    return hi, (x - hi.astype(F32)).astype(BF16)


def put(ref, base, rows, cols, re, im):
    for i, x in enumerate((re, im, re + im)):
        hi, lo = halves(x)
        ref[base + 2 * i, rows, cols] = hi
        ref[base + 2 * i + 1, rows, cols] = lo


def split(net, gather, mats, row_base):
    for k in range(2):
        axes = [[(p + q + k + gather.group) % 3 for q in range(3)] for p in range(3)]

        def body(i, _, k=k, axes=axes):
            far = (i % 4, (i // 4) % 4, i // 16)
            at = [(net.pos[a] + far[a]) % 4 for a in range(3)]
            row = (at[2] % 2) * 8 + at[0] * 2 + k
            col = at[1] * 2 + at[2] // 2
            src = [((k * 4 + far[a3]) * 4 + far[a2]) * 4 + far[a1] for a1, a2, a3 in axes]
            cols = pl.ds(pl.multiple_of(col * 128, 128), 128)
            tile = [gather.bufs[p][src[p], g] for p, g in GRANULE]
            for t in range(2):
                re = jnp.concatenate([tile[2 * t], tile[2 * t + 1]], 0)
                im = jnp.concatenate([tile[4 + 2 * t], tile[5 + 2 * t]], 0)
                rows = pl.ds(pl.multiple_of(row_base + row * 32 + t * 16, 16), 16)
                put(mats, 0, rows, cols, re, im)
            return 0

        lax.fori_loop(0, 64, body, 0, unroll=2)


def product(mats, rows, z, base):
    dot = functools.partial(jnp.dot, preferred_element_type=F32)
    out = []
    for i in range(3):
        a_hi, a_lo = mats[2 * i, rows, :], mats[2 * i + 1, rows, :]
        z_hi, z_lo = z[base + 2 * i], z[base + 2 * i + 1]
        out.append(dot(a_hi, z_hi) + (dot(a_hi, z_lo) + dot(a_lo, z_hi)))
    return out[0] - out[1], out[2] - out[0] - out[1]


def wide(x):
    return jnp.concatenate([x, x], 1)


def kernel(frf, mount, recv_rows, codes, stiffness, loss, load, out, frf_v, *refs):
    h0, h1, rb = refs[0:3], refs[3:6], refs[6:9]
    amat, rmat, z, delta, load_c, y1_c, picked, sum1, got1, got2, got3, y1_own, y1_part, y1_sum, y1_all = refs[9:24]
    send, recv, misc_send, misc_recv, local = refs[24:]
    net = Net()
    k = net.k
    whole = pltpu.make_async_copy(frf, frf_v, local)
    whole.start()
    net.greet()
    lane = lax.broadcasted_iota(jnp.int32, (8, 128), 1)
    sub = lax.broadcasted_iota(jnp.int32, (8, 128), 0)

    def column(tile, at):
        return jnp.broadcast_to(jnp.sum(jnp.where(lane == sub + at, tile, 0.0), axis=1, keepdims=True), (8, 128))

    gathers = [Gather(i, bufs, send, recv, net, picked) for i, bufs in enumerate((h0, h1, rb))]
    whole.wait()

    first_row = net.r * 4096
    cols = pl.ds(pl.multiple_of(net.v * 128, 128), 128)
    l_re = jnp.broadcast_to(load[0:1, cols], (8, 128))
    l_im = jnp.broadcast_to(load[1:2, cols], (8, 128))
    part = jnp.zeros((8, 128), F32)
    for t in range(8):
        at = [jnp.clip(mount[net.r * 64 + t * 8 + s] - first_row, 0, 4095) for s in range(8)]
        re, im = (jnp.concatenate([frf_v[c, pl.ds(i, 1), :] for i in at], 0) for c in range(2))
        for c, x in ((0, re), (1, im)):
            p, g = GRANULE[c * 4 + t % 4]
            (h0, h1)[t // 4][p][k * 64, g] = x
        y_re = jnp.sum(re * l_re - im * l_im, axis=1, keepdims=True)
        y_im = jnp.sum(re * l_im + im * l_re, axis=1, keepdims=True)
        part = part + jnp.where(lane == sub + t * 8, y_re, 0.0) + jnp.where(lane == sub + 64 + t * 8, y_im, 0.0)
    y1_own[0] = part
    net.greeted()

    def spread(src, dst, i, devs):
        for n, dev in enumerate(devs):
            pltpu.make_async_remote_copy(
                src_ref=src.at[0], dst_ref=dst.at[n], send_sem=misc_send.at[i], recv_sem=misc_recv.at[i],
                device_id=dev, device_id_type=MESH).start()

    def settle(ref, i):
        pltpu.make_async_copy(ref, ref, misc_send.at[i]).wait()

    def arrive(ref, i):
        pltpu.make_async_copy(ref, ref, misc_recv.at[i]).wait()

    spread(y1_own, y1_part, 0, net.same_row)
    gathers[0].first()
    gathers[1].first()

    def pick(b, _):
        zl, x, kk = b // 8, (b // 2) % 4, b % 2
        to = (kk * 4 + x) * 2 + zl
        for t in range(4):
            at = [recv_rows[b * 32 + t * 8 + s] - first_row for s in range(8)]
            inside = [(i >= 0) & (i < 4096) for i in at]
            at = [jnp.clip(i, 0, 4095) for i in at]
            for c in range(2):
                x8 = [jnp.where(inside[s], frf_v[c, pl.ds(at[s], 1), :], 0.0) for s in range(8)]
                picked[to, c * 4 + t] = jnp.concatenate(x8, 0)
        return 0

    lax.fori_loop(0, 16, pick, 0)
    mine, other = pl.ds(k * 8, 8), pl.ds((1 - k) * 8, 8)
    pltpu.make_async_remote_copy(
        src_ref=picked.at[other], dst_ref=got1, send_sem=misc_send.at[2], recv_sem=misc_recv.at[2],
        device_id=net.sib, device_id_type=MESH).start()

    gathers[0].second()
    gathers[1].second()

    arrive(y1_part, 0)
    total = y1_own[0]
    for i in range(7):
        total = total + y1_part[i]
    y1_sum[0] = total
    spread(y1_sum, y1_all, 1, net.same_var)

    arrive(got1, 2)
    sum1[...] = picked[mine] + got1[...]
    xx = net.pos[0]
    for n, d in enumerate((1, 2, 3)):
        pltpu.make_async_remote_copy(
            src_ref=sum1.at[pl.ds(((xx + d) % 4) * 2, 2)], dst_ref=got2.at[pl.ds(n * 2, 2)],
            send_sem=misc_send.at[3], recv_sem=misc_recv.at[3], device_id=net.near[0, d], device_id_type=MESH).start()

    for d in ORDER:
        gathers[0].third(d)
    for d in ORDER:
        gathers[1].third(d)

    arrive(got2, 3)
    sums = [sum1[xx * 2 + i] + got2[i] + got2[2 + i] + got2[4 + i] for i in range(2)]
    for i in range(2):
        got1[i] = sums[i]
    pltpu.make_async_remote_copy(
        src_ref=got1.at[1 - net.zl], dst_ref=got3, send_sem=misc_send.at[4], recv_sem=misc_recv.at[4],
        device_id=net.pair, device_id_type=MESH).start()

    def load_columns(j, _):
        rows = pl.ds(pl.multiple_of(j * 8, 8), 8)
        c128 = pl.ds(pl.multiple_of((j // 16) * 128, 128), 128)
        for c in range(2):
            load_c[c, rows, :] = column(jnp.broadcast_to(load[c : c + 1, c128], (8, 128)), (j % 16) * 8)
        return 0

    lax.fori_loop(0, 128, load_columns, 0)

    def table(ref):
        quarter = lax.broadcasted_iota(jnp.int32, (8, 256), 0) % 4
        out = []
        for l in range(LEVELS):
            x = jnp.where(quarter == 0, ref[l, 0], ref[l, 1])
            out.append(jnp.where(quarter == 2, ref[l, 2], jnp.where(quarter == 3, ref[l, 3], x)))
        return out

    code_b = codes[...].astype(F32).astype(BF16)
    for b in range(4):
        mount_of = lax.broadcasted_iota(jnp.int32, (256, 256), 0) // 4 + b * 64
        rep = (mount_of == lax.broadcasted_iota(jnp.int32, (256, 256), 1)).astype(F32).astype(BF16)
        delta[0, pl.ds(b * 256, 256), :] = lax.dot_general(rep, code_b, (((1,), (1,)), ((), ())), preferred_element_type=F32)
    stiff_t, loss_t = table(stiffness), table(loss)

    def look(j, _):
        rows = pl.ds(pl.multiple_of(j * 8, 8), 8)
        code = delta[0, rows, :]
        s, e = stiff_t[0], loss_t[0]
        for l in range(1, LEVELS):
            here = code == float(l)
            s, e = jnp.where(here, stiff_t[l], s), jnp.where(here, loss_t[l], e)
        delta[0, rows, :] = s
        delta[1, rows, :] = s * e
        return 0

    lax.fori_loop(0, 128, look, 0)

    arrive(y1_all, 1)
    y1_c[pl.ds(net.r * 8, 8), :] = y1_sum[0]
    for i in range(15):
        y1_c[pl.ds(((net.r + 15 - i) % 16) * 8, 8), :] = y1_all[i]

    def step(rows, y_re, y_im, to):
        d_re, d_im = delta[0, rows, :], delta[1, rows, :]
        z_re = wide(load_c[0, rows, :]) - (d_re * y_re - d_im * y_im)
        z_im = wide(load_c[1, rows, :]) - (d_re * y_im + d_im * y_re)
        put(z, to, rows, slice(None), z_re, z_im)

    def begin(j, _):
        tile = y1_c[pl.ds(pl.multiple_of((j // 4) * 8, 8), 8), :]
        at = (j % 4) * 16
        y_re, y_im = (jnp.concatenate([column(tile, at + 64 * c), column(tile, at + 64 * c + 8)], 0) for c in range(2))
        step(pl.ds(pl.multiple_of(j * 16, 16), 16), wide(y_re), wide(y_im), 0)
        return 0

    lax.fori_loop(0, 64, begin, 0)

    gathers[0].lasts(0, 3, 1, 2)
    gathers[1].lasts(0, 3, 1, 2)

    arrive(got3, 4)
    share = got1[net.zl] + got3[...]
    for i, (p, g) in enumerate(GRANULE):
        rb[p][k * 64, g] = share[i]
    gathers[2].first()

    gathers[0].cores()
    split(net, gathers[0], amat, 0)
    gathers[2].second()
    gathers[1].cores()
    split(net, gathers[1], amat, 512)
    for d in ORDER:
        gathers[2].third(d)

    def iterate(b, frm, to):
        y_re, y_im = product(amat, pl.ds(pl.multiple_of(b * 256, 256), 256), z, frm)
        for j in range(8):
            here = slice(j * 32, j * 32 + 32)
            rows = pl.ds(pl.multiple_of(((b % 2) * 8 + j) * 64 + (b // 2) * 32, 32), 32)
            step(rows, y_re[here], y_im[here], to)

    for it in range(1, ITERS):
        frm, to = (0, 6) if it % 2 == 1 else (6, 0)

        def block(b, _, frm=frm, to=to):
            iterate(b, frm, to)
            return 0

        lax.fori_loop(0, 4, block, 0)
        if it == 1:
            gathers[2].lasts(0, 3)
        elif it == 2:
            gathers[2].lasts(1, 2)

    gathers[2].cores()
    split(net, gathers[2], rmat, 0)

    def answer(b, _):
        o_re, o_im = product(rmat, pl.ds(pl.multiple_of(b * 256, 256), 256), z, 6)
        cols = pl.ds(pl.multiple_of(b * 256, 256), 256)
        out[0, :, cols] = o_re.T
        out[1, :, cols] = o_im.T
        return 0

    lax.fori_loop(0, 2, answer, 0)

    settle(y1_part, 0)
    settle(y1_all, 1)
    settle(got1, 2)
    settle(got2, 3)
    settle(got3, 4)
    for g in gathers:
        g.end(frf_v)


def on_device(frf, mount_rows, recv_rows, codes, stiffness, loss, load):
    vmem, smem = pl.BlockSpec(memory_space=pltpu.VMEM), pl.BlockSpec(memory_space=pltpu.SMEM)
    count = codes.shape[0]
    tile = (8, 128)
    return pl.pallas_call(
        kernel,
        out_shape=jax.ShapeDtypeStruct((2, count, recv_rows.shape[0]), F32),
        in_specs=[pl.BlockSpec(memory_space=pl.ANY), smem, smem, vmem, smem, smem, vmem],
        out_specs=vmem,
        scratch_shapes=[pltpu.VMEM(frf.shape, F32)]
        + [pltpu.VMEM((128, n) + tile, F32) for n in PART * 3]
        + [
            pltpu.VMEM((6, 1024, 1024), BF16),
            pltpu.VMEM((6, 512, 1024), BF16),
            pltpu.VMEM((12, 1024, count), BF16),
            pltpu.VMEM((2, 1024, count), F32),
            pltpu.VMEM((2, 1024, 128), F32),
            pltpu.VMEM((128, 128), F32),
            pltpu.VMEM((16, 8) + tile, F32),
            pltpu.VMEM((8, 8) + tile, F32),
            pltpu.VMEM((8, 8) + tile, F32),
            pltpu.VMEM((6, 8) + tile, F32),
            pltpu.VMEM((8,) + tile, F32),
            pltpu.VMEM((1,) + tile, F32),
            pltpu.VMEM((7,) + tile, F32),
            pltpu.VMEM((1,) + tile, F32),
            pltpu.VMEM((15,) + tile, F32),
            pltpu.SemaphoreType.DMA((3,)),
            pltpu.SemaphoreType.DMA((3 * NREC,)),
            pltpu.SemaphoreType.DMA((5,)),
            pltpu.SemaphoreType.DMA((5,)),
            pltpu.SemaphoreType.DMA,
        ],
        compiler_params=pltpu.CompilerParams(collective_id=0, has_side_effects=True, vmem_limit_bytes=58 * 2**20),
        cost_estimate=pl.CostEstimate(flops=int(1.7e10), bytes_accessed=2**23, transcendentals=0),
    )(frf, mount_rows.reshape(-1), recv_rows, codes, stiffness, loss, load)


def solution(mesh):
    placed = (P(None, "row", "var"), P(), P(), P(("var", "row"), None), P(), P(), P())
    return jax.shard_map(
        on_device,
        mesh=mesh,
        in_specs=placed,
        out_specs=P(None, ("var", "row"), None),
        check_vma=False,
    )
```

```python
import functools

import jax
import jax.numpy as jnp
from jax import lax
from jax.experimental import pallas as pl
from jax.experimental.pallas import tpu as pltpu
from jax.sharding import PartitionSpec as P

MESH = pl.DeviceIdType.MESH
F32, BF16 = jnp.float32, jnp.bfloat16
ITERS = 4
LEVELS = 8
GRANULE = ((0, 0), (0, 1), (0, 2), (1, 0), (1, 1), (1, 2), (2, 0), (2, 1))
PART = (3, 3, 2)
ORDER = (1, 3, 2)
NREC = 20


def device(x, y, z, k):
    return {"var": y * 2 + z // 2, "row": (z % 2) * 8 + x * 2 + k}


class Net:
    def __init__(self):
        v, r = lax.axis_index("var"), lax.axis_index("row")
        y, zh = v // 2, v % 2
        zl, x, k = r // 8, (r // 2) % 4, r % 2
        z = zh * 2 + zl
        self.v, self.r, self.zl, self.zh, self.k = v, r, zl, zh, k
        self.pos = (x, y, z)
        self.near = {}
        for a in range(3):
            for d in (1, 2, 3):
                c = [x, y, z]
                c[a] = (c[a] + d) % 4
                self.near[a, d] = device(*c, k)
        self.sib = device(x, y, z, 1 - k)
        self.pair = {"var": v, "row": (1 - zl) * 8 + x * 2 + k}
        self.same_row = [{"var": (v + i) % 8, "row": r} for i in range(1, 8)]
        self.same_var = [{"var": v, "row": (r + i) % 16} for i in range(1, 16)]

    def along(self, turn, d):
        m, n = self.near[turn % 3, d], self.near[(turn + 1) % 3, d]
        return {q: jnp.where(self.k == 0, m[q], n[q]) for q in ("var", "row")}

    def greet(self):
        sem = pltpu.get_barrier_semaphore()
        for d in list(self.near.values()) + self.same_row + self.same_var:
            pl.semaphore_signal(sem, inc=1, device_id=d, device_id_type=MESH)

    def greeted(self):
        pl.semaphore_wait(pltpu.get_barrier_semaphore(), 9 + 7 + 15)


def slot(k, d3, d2, d1=0, n=1):
    return pl.ds(((k * 4 + d3) * 4 + d2) * 4 + d1, n)


class Gather:
    def __init__(self, group, bufs, send, recv, net, size_ref):
        self.group, self.bufs, self.net, self.size_ref = group, bufs, net, size_ref
        self.send, self.recv = send.at[group], recv
        self.count = 0

    def sem(self, kind, i=0):
        return self.recv.at[self.group * NREC + {"a": 0, "b": 0, "c": 4, "s": 16}[kind] + i]

    def go(self, p, src, dst, sem, dev):
        pltpu.make_async_remote_copy(
            src_ref=self.bufs[p].at[src], dst_ref=self.bufs[p].at[dst], send_sem=self.send, recv_sem=sem,
            device_id=dev, device_id_type=MESH).start()

    def wait(self, n, sem):
        ref = self.size_ref.at[pl.ds(0, n)]
        pltpu.make_async_copy(ref, ref, sem).wait()

    def dev(self, p, axis, d):
        return self.net.along(p + axis - 1 + self.group, d)

    def first(self):
        k = self.net.k
        for p in range(3):
            for d in ORDER:
                self.go(p, slot(k, 0, 0), slot(k, 0, 0, 4 - d), self.sem("a"), self.dev(p, 1, d))
        for p in range(3):
            self.send_b(p, (0, 1))
        for p in range(3):
            self.send_c(p, 0, (0, 1))

    def send_b(self, p, what):
        k = self.net.k
        for d in ORDER:
            self.go(p, slot(k, 0, 0, *what), slot(k, 0, 4 - d, *what), self.sem("b", d), self.dev(p, 2, d))

    def send_c(self, p, d2, what):
        k = self.net.k
        for d in ORDER:
            self.go(p, slot(k, 0, d2, *what), slot(k, 4 - d, d2, *what), self.sem("c", d2 * 3 + d - 1), self.dev(p, 3, d))

    def core(self, d3, d2):
        at = slot(self.net.k, d3, d2, 0, 4)
        for p in range(3):
            self.go(p, at, at, self.sem("s", d3), self.net.sib)

    def second(self):
        self.wait(3, self.sem("a"))
        for p in range(3):
            self.send_b(p, (1, 3))
        for p in range(3):
            self.send_c(p, 0, (1, 3))
        self.core(0, 0)

    def third(self, d):
        self.wait(4, self.sem("b", d))
        for p in range(3):
            self.send_c(p, 4 - d, (0, 4))
        self.core(0, 4 - d)

    def last(self, d2, d):
        self.wait(4, self.sem("c", d2 * 3 + d - 1))
        self.core(4 - d, d2)

    def lasts(self, *lines):
        for d2 in lines:
            for d in ORDER:
                self.last(d2, d)

    def cores(self):
        for d3 in range(4):
            self.wait(16, self.sem("s", d3))

    def end(self, frf_v):
        ref = frf_v.at[:, pl.ds(0, 127 * 32), :]
        pltpu.make_async_copy(ref, ref, self.send).wait()


def halves(x):
    hi = x.astype(BF16)
    return hi, (x - hi.astype(F32)).astype(BF16)


def put(ref, at, re, im):
    for i, x in enumerate((re, im, re + im)):
        hi, lo = halves(x)
        ref[at(2 * i)] = hi
        ref[at(2 * i + 1)] = lo


def split(net, gather, mats, row_base, cores=(0, 1)):
    for kk in cores:
        own = [[(p + q + kk + gather.group) % 3 for q in range(3)] for p in range(3)]
        def add(p, a, c):
            return ((c - net.pos[a] + 4) % 4) * 4 ** own[p].index(a)

        xs = [[add(p, 0, x) + kk * 64 for x in range(4)] for p in range(3)]
        zs = [[add(p, 2, z) for z in range(4)] for p in range(3)]

        def body(y, _, kk=kk, xs=xs, zs=zs, add=add):
            ys = [add(p, 1, y) for p in range(3)]
            for z in range(4):
                yz = [ys[p] + zs[p][z] for p in range(3)]
                col = y * 2 + z // 2
                for x in range(4):
                    src = [yz[p] + xs[p][x] for p in range(3)]
                    tile = [gather.bufs[p][src[p], g] for p, g in GRANULE]
                    for t in range(2):
                        re = jnp.concatenate([tile[2 * t], tile[2 * t + 1]], 0)
                        im = jnp.concatenate([tile[4 + 2 * t], tile[5 + 2 * t]], 0)
                        first = row_base + (kk * 8 + (z % 2) * 4 + x) * 32 + t * 16
                        put(mats, lambda i: (i, col, pl.ds(first, 16)), re, im)
            return 0

        lax.fori_loop(0, 4, body, 0)


def product(mats, rows, z, base):
    dot = functools.partial(jnp.dot, preferred_element_type=F32)
    out = []
    for i in range(3):
        a_hi, a_lo = (jnp.concatenate([mats[2 * i + n, c, rows, :] for c in range(8)], 1) for n in range(2))
        z_hi, z_lo = z[base + 2 * i], z[base + 2 * i + 1]
        out.append(dot(a_hi, z_hi) + (dot(a_hi, z_lo) + dot(a_lo, z_hi)))
    return out[0] - out[1], out[2] - out[0] - out[1]


def wide(x):
    return jnp.concatenate([x, x], 1)


def kernel(frf, mount, recv_rows, codes, stiffness, loss, load, out, frf_v, *refs):
    h0, h1, rb = refs[0:3], refs[3:6], refs[6:9]
    amat, rmat, z, delta, load_c, y1_c, picked, sum1, got1, got2, got3, y1_own, y1_part, y1_sum, y1_all, found = refs[9:25]
    send, recv, misc_send, misc_recv, local = refs[25:]
    net = Net()
    k = net.k
    whole = pltpu.make_async_copy(frf, frf_v, local)
    whole.start()
    net.greet()
    lane = lax.broadcasted_iota(jnp.int32, (8, 128), 1)
    sub = lax.broadcasted_iota(jnp.int32, (8, 128), 0)

    gathers = [Gather(i, bufs, send, recv, net, picked) for i, bufs in enumerate((h0, h1, rb))]
    whole.wait()

    first_row = net.r * 4096
    cols = pl.ds(pl.multiple_of(net.v * 128, 128), 128)
    l_re = jnp.broadcast_to(load[0:1, cols], (8, 128))
    l_im = jnp.broadcast_to(load[1:2, cols], (8, 128))
    part = jnp.zeros((8, 128), F32)
    for t in range(8):
        at = [jnp.clip(mount[net.r * 64 + t * 8 + s] - first_row, 0, 4095) for s in range(8)]
        re, im = (jnp.concatenate([frf_v[c, pl.ds(i, 1), :] for i in at], 0) for c in range(2))
        for c, x in ((0, re), (1, im)):
            p, g = GRANULE[c * 4 + t % 4]
            (h0, h1)[t // 4][p][k * 64, g] = x
        y_re = jnp.sum(re * l_re - im * l_im, axis=1, keepdims=True)
        y_im = jnp.sum(re * l_im + im * l_re, axis=1, keepdims=True)
        part = part + jnp.where(lane == sub + t * 8, y_re, 0.0) + jnp.where(lane == sub + 64 + t * 8, y_im, 0.0)
    y1_own[0] = part
    net.greeted()

    def spread(src, dst, i, devs):
        for n, dev in enumerate(devs):
            pltpu.make_async_remote_copy(
                src_ref=src.at[0], dst_ref=dst.at[n], send_sem=misc_send.at[i], recv_sem=misc_recv.at[i],
                device_id=dev, device_id_type=MESH).start()

    def settle(ref, i):
        pltpu.make_async_copy(ref, ref, misc_send.at[i]).wait()

    def arrive(ref, i):
        pltpu.make_async_copy(ref, ref, misc_recv.at[i]).wait()

    spread(y1_own, y1_part, 0, net.same_row)
    gathers[0].first()
    gathers[1].first()

    def pick(b, _):
        zl, x, kk = b // 8, (b // 2) % 4, b % 2
        to = (kk * 4 + x) * 2 + zl
        for t in range(4):
            at = [recv_rows[b * 32 + t * 8 + s] - first_row for s in range(8)]
            inside = [(i >= 0) & (i < 4096) for i in at]
            at = [jnp.clip(i, 0, 4095) for i in at]
            for c in range(2):
                x8 = [jnp.where(inside[s], frf_v[c, pl.ds(at[s], 1), :], 0.0) for s in range(8)]
                picked[to, c * 4 + t] = jnp.concatenate(x8, 0)
        return 0

    lax.fori_loop(0, 16, pick, 0)
    mine, other = pl.ds(k * 8, 8), pl.ds((1 - k) * 8, 8)
    pltpu.make_async_remote_copy(
        src_ref=picked.at[other], dst_ref=got1, send_sem=misc_send.at[2], recv_sem=misc_recv.at[2],
        device_id=net.sib, device_id_type=MESH).start()

    code_b = codes[...].astype(F32).astype(BF16)
    for b in range(4):
        mount_of = lax.broadcasted_iota(jnp.int32, (256, 256), 0) // 4 + b * 64
        rep = (mount_of == lax.broadcasted_iota(jnp.int32, (256, 256), 1)).astype(F32).astype(BF16)
        delta[0, pl.ds(b * 256, 256), :] = lax.dot_general(rep, code_b, (((1,), (1,)), ((), ())), preferred_element_type=F32)

    gathers[0].second()
    gathers[1].second()

    arrive(y1_part, 0)
    total = y1_own[0]
    for i in range(7):
        total = total + y1_part[i]
    y1_sum[0] = total
    spread(y1_sum, y1_all, 1, net.same_var)

    arrive(got1, 2)
    sum1[...] = picked[mine] + got1[...]
    xx = net.pos[0]
    for n, d in enumerate((1, 2, 3)):
        pltpu.make_async_remote_copy(
            src_ref=sum1.at[pl.ds(((xx + d) % 4) * 2, 2)], dst_ref=got2.at[pl.ds(n * 2, 2)],
            send_sem=misc_send.at[3], recv_sem=misc_recv.at[3], device_id=net.near[0, d], device_id_type=MESH).start()

    for d in ORDER:
        gathers[0].third(d)
    for d in ORDER:
        gathers[1].third(d)

    for b in range(8):
        at = pl.ds(b * 128, 128)
        for c in range(2):
            load_c[c, at, :] = jnp.broadcast_to(load[c : c + 1, at], (128, 128)).T

    def table(ref):
        quarter = lax.broadcasted_iota(jnp.int32, (8, 256), 0) % 4
        out = []
        for l in range(LEVELS):
            x = jnp.where(quarter == 0, ref[l, 0], ref[l, 1])
            out.append(jnp.where(quarter == 2, ref[l, 2], jnp.where(quarter == 3, ref[l, 3], x)))
        return out

    stiff_t, loss_t = table(stiffness), table(loss)

    def look(j, _):
        rows = pl.ds(pl.multiple_of(j * 8, 8), 8)
        code = delta[0, rows, :]
        s, e = stiff_t[0], loss_t[0]
        for l in range(1, LEVELS):
            here = code == float(l)
            s, e = jnp.where(here, stiff_t[l], s), jnp.where(here, loss_t[l], e)
        delta[0, rows, :] = s
        delta[1, rows, :] = s * e
        return 0

    lax.fori_loop(0, 128, look, 0, unroll=4)

    def step(rows, y_re, y_im, to):
        d_re, d_im = delta[0, rows, :], delta[1, rows, :]
        z_re = wide(load_c[0, rows, :]) - (d_re * y_re - d_im * y_im)
        z_im = wide(load_c[1, rows, :]) - (d_re * y_im + d_im * y_re)
        put(z, lambda i: (to + i, rows), z_re, z_im)

    gathers[0].lasts(0)

    arrive(got2, 3)
    sums = [sum1[xx * 2 + i] + got2[i] + got2[2 + i] + got2[4 + i] for i in range(2)]
    for i in range(2):
        got1[i] = sums[i]
    pltpu.make_async_remote_copy(
        src_ref=got1.at[1 - net.zl], dst_ref=got3, send_sem=misc_send.at[4], recv_sem=misc_recv.at[4],
        device_id=net.pair, device_id_type=MESH).start()

    gathers[0].lasts(3)

    arrive(y1_all, 1)
    y1_c[pl.ds(net.r * 8, 8), :] = y1_sum[0]
    for i in range(15):
        y1_c[pl.ds(((net.r + 15 - i) % 16) * 8, 8), :] = y1_all[i]

    def begin(j, _):
        tile = y1_c[pl.ds(pl.multiple_of(j * 8, 8), 8), :]
        both = jnp.broadcast_to(jnp.sum(tile, axis=0, keepdims=True), (128, 128)).T
        for i in range(2):
            step(pl.ds(pl.multiple_of(j * 64 + i * 32, 32), 32), wide(both[i * 32 : i * 32 + 32]), wide(both[64 + i * 32 : 96 + i * 32]), 0)
        return 0

    lax.fori_loop(0, 16, begin, 0)

    gathers[0].lasts(1)
    arrive(got3, 4)
    share = got1[net.zl] + got3[...]
    for i, (p, g) in enumerate(GRANULE):
        rb[p][k * 64, g] = share[i]
    gathers[2].first()
    gathers[0].lasts(2)

    def iterate(first, count, frm, to):
        y_re, y_im = product(amat, pl.ds(first, count), z, frm)
        for j in range(count // 32):
            here = slice(j * 32, j * 32 + 32)
            h, i = (first // 32 + j) // 16, (first // 32 + j) % 16
            kk, zl, x = i // 8, (i // 4) % 2, i % 4
            rows = pl.ds((zl * 8 + x * 2 + kk) * 64 + h * 32, 32)
            step(rows, y_re[here], y_im[here], to)

    gathers[1].lasts(0)
    gathers[0].cores()
    gathers[2].second()
    split(net, gathers[0], amat, 0)
    gathers[1].lasts(3, 1)
    for d in ORDER:
        gathers[2].third(d)
    iterate(0, 512, 0, 6)
    gathers[1].lasts(2)
    gathers[1].cores()
    split(net, gathers[1], amat, 512)
    iterate(512, 512, 0, 6)
    gathers[2].lasts(0, 3, 1, 2)

    def again(it, _):
        iterate(0, 1024, 6 - it * 6, it * 6)
        return 0

    lax.fori_loop(0, ITERS - 2, again, 0)

    gathers[2].cores()
    split(net, gathers[2], rmat, 0)

    def answer(kk, _):
        parts = product(rmat, pl.ds(pl.multiple_of(kk * 256, 256), 256), z, 6)
        for c in range(2):
            for i in range(8):
                found[c, pl.ds(pl.multiple_of(i * 64 + kk * 32, 32), 32), :] = parts[c][i * 32 : i * 32 + 32]
        return 0

    lax.fori_loop(0, 2, answer, 0)
    for c in range(2):
        for b in range(2):
            out[c, :, pl.ds(b * 256, 256)] = found[c, pl.ds(b * 256, 256), :].T

    settle(y1_part, 0)
    settle(y1_all, 1)
    settle(got1, 2)
    settle(got2, 3)
    settle(got3, 4)
    for g in gathers:
        g.end(frf_v)


def on_device(frf, mount_rows, recv_rows, codes, stiffness, loss, load):
    vmem, smem = pl.BlockSpec(memory_space=pltpu.VMEM), pl.BlockSpec(memory_space=pltpu.SMEM)
    count = codes.shape[0]
    tile = (8, 128)
    return pl.pallas_call(
        kernel,
        out_shape=jax.ShapeDtypeStruct((2, count, recv_rows.shape[0]), F32),
        in_specs=[pl.BlockSpec(memory_space=pl.ANY), smem, smem, vmem, smem, smem, vmem],
        out_specs=vmem,
        scratch_shapes=[pltpu.VMEM(frf.shape, F32)]
        + [pltpu.VMEM((128, n) + tile, F32) for n in PART * 3]
        + [
            pltpu.VMEM((6, 8, 1024, 128), BF16),
            pltpu.VMEM((6, 8, 512, 128), BF16),
            pltpu.VMEM((12, 1024, count), BF16),
            pltpu.VMEM((2, 1024, count), F32),
            pltpu.VMEM((2, 1024, 128), F32),
            pltpu.VMEM((128, 128), F32),
            pltpu.VMEM((16, 8) + tile, F32),
            pltpu.VMEM((8, 8) + tile, F32),
            pltpu.VMEM((8, 8) + tile, F32),
            pltpu.VMEM((6, 8) + tile, F32),
            pltpu.VMEM((8,) + tile, F32),
            pltpu.VMEM((1,) + tile, F32),
            pltpu.VMEM((7,) + tile, F32),
            pltpu.VMEM((1,) + tile, F32),
            pltpu.VMEM((15,) + tile, F32),
            pltpu.VMEM((2, 512, count), F32),
            pltpu.SemaphoreType.DMA((3,)),
            pltpu.SemaphoreType.DMA((3 * NREC,)),
            pltpu.SemaphoreType.DMA((5,)),
            pltpu.SemaphoreType.DMA((5,)),
            pltpu.SemaphoreType.DMA,
        ],
        compiler_params=pltpu.CompilerParams(collective_id=0, has_side_effects=True, vmem_limit_bytes=58 * 2**20),
        cost_estimate=pl.CostEstimate(flops=int(1.7e10), bytes_accessed=2**23, transcendentals=0),
    )(frf, mount_rows.reshape(-1), recv_rows, codes, stiffness, loss, load)


def solution(mesh):
    placed = (P(None, "row", "var"), P(), P(), P(("var", "row"), None), P(), P(), P())
    return jax.shard_map(
        on_device,
        mesh=mesh,
        in_specs=placed,
        out_specs=P(None, ("var", "row"), None),
        check_vma=False,
    )
```

```python
import functools

import jax
import jax.numpy as jnp
from jax import lax
from jax.experimental import pallas as pl
from jax.experimental.pallas import tpu as pltpu
from jax.sharding import PartitionSpec as P

MESH = pl.DeviceIdType.MESH
F32, BF16 = jnp.float32, jnp.bfloat16
ITERS = 4
LEVELS = 8
GRANULE = ((0, 0), (0, 1), (0, 2), (1, 0), (1, 1), (1, 2), (2, 0), (2, 1))
PART = (3, 3, 2)
ORDER = (1, 3, 2)
NREC = 20


def device(x, y, z, k):
    return {"var": y * 2 + z // 2, "row": (z % 2) * 8 + x * 2 + k}


class Net:
    def __init__(self):
        v, r = lax.axis_index("var"), lax.axis_index("row")
        y, zh = v // 2, v % 2
        zl, x, k = r // 8, (r // 2) % 4, r % 2
        z = zh * 2 + zl
        self.v, self.r, self.zl, self.zh, self.k = v, r, zl, zh, k
        self.pos = (x, y, z)
        self.near = {}
        for a in range(3):
            for d in (1, 2, 3):
                c = [x, y, z]
                c[a] = (c[a] + d) % 4
                self.near[a, d] = device(*c, k)
        self.sib = device(x, y, z, 1 - k)
        self.pair = {"var": v, "row": (1 - zl) * 8 + x * 2 + k}
        self.same_row = [{"var": (v + i) % 8, "row": r} for i in range(1, 8)]
        self.same_var = [{"var": v, "row": (r + i) % 16} for i in range(1, 16)]

    def along(self, turn, d):
        m, n = self.near[turn % 3, d], self.near[(turn + 1) % 3, d]
        return {q: jnp.where(self.k == 0, m[q], n[q]) for q in ("var", "row")}

    def greet(self):
        sem = pltpu.get_barrier_semaphore()
        for d in list(self.near.values()) + self.same_row + self.same_var:
            pl.semaphore_signal(sem, inc=1, device_id=d, device_id_type=MESH)

    def greeted(self):
        pl.semaphore_wait(pltpu.get_barrier_semaphore(), 9 + 7 + 15)


def slot(k, d3, d2, d1=0, n=1):
    return pl.ds(((k * 4 + d3) * 4 + d2) * 4 + d1, n)


class Gather:
    def __init__(self, group, bufs, send, recv, net, size_ref):
        self.group, self.bufs, self.net, self.size_ref = group, bufs, net, size_ref
        self.send, self.recv = send.at[group], recv
        self.count = 0

    def sem(self, kind, i=0):
        return self.recv.at[self.group * NREC + {"a": 0, "b": 0, "c": 4, "s": 16}[kind] + i]

    def go(self, p, src, dst, sem, dev):
        pltpu.make_async_remote_copy(
            src_ref=self.bufs[p].at[src], dst_ref=self.bufs[p].at[dst], send_sem=self.send, recv_sem=sem,
            device_id=dev, device_id_type=MESH).start()

    def wait(self, n, sem):
        ref = self.size_ref.at[pl.ds(0, n)]
        pltpu.make_async_copy(ref, ref, sem).wait()

    def dev(self, p, axis, d):
        return self.net.along(p + axis - 1 + self.group, d)

    def first(self):
        k = self.net.k
        for p in range(3):
            for d in ORDER:
                self.go(p, slot(k, 0, 0), slot(k, 0, 0, 4 - d), self.sem("a"), self.dev(p, 1, d))
        for p in range(3):
            self.send_b(p, (0, 1))
        for p in range(3):
            self.send_c(p, 0, (0, 1))

    def send_b(self, p, what):
        k = self.net.k
        for d in ORDER:
            self.go(p, slot(k, 0, 0, *what), slot(k, 0, 4 - d, *what), self.sem("b", d), self.dev(p, 2, d))

    def send_c(self, p, d2, what):
        k = self.net.k
        for d in ORDER:
            self.go(p, slot(k, 0, d2, *what), slot(k, 4 - d, d2, *what), self.sem("c", d2 * 3 + d - 1), self.dev(p, 3, d))

    def core(self, d3, d2):
        at = slot(self.net.k, d3, d2, 0, 4)
        for p in range(3):
            self.go(p, at, at, self.sem("s", d3), self.net.sib)

    def second(self):
        self.wait(3, self.sem("a"))
        for p in range(3):
            self.send_b(p, (1, 3))
        for p in range(3):
            self.send_c(p, 0, (1, 3))
        self.core(0, 0)

    def third(self, d):
        self.wait(4, self.sem("b", d))
        for p in range(3):
            self.send_c(p, 4 - d, (0, 4))
        self.core(0, 4 - d)

    def last(self, d2, d):
        self.wait(4, self.sem("c", d2 * 3 + d - 1))
        self.core(4 - d, d2)

    def lasts(self, *lines):
        for d2 in lines:
            for d in ORDER:
                self.last(d2, d)

    def cores(self):
        for d3 in range(4):
            self.wait(16, self.sem("s", d3))

    def end(self, frf_v):
        ref = frf_v.at[:, pl.ds(0, 127 * 32), :]
        pltpu.make_async_copy(ref, ref, self.send).wait()


def halves(x):
    hi = x.astype(BF16)
    return hi, (x - hi.astype(F32)).astype(BF16)


def put(ref, at, re, im):
    for i, x in enumerate((re, im, re + im)):
        hi, lo = halves(x)
        ref[at(2 * i)] = hi
        ref[at(2 * i + 1)] = lo


def split(net, gather, mats, row_base, cores=(0, 1)):
    for kk in cores:
        own = [[(p + q + kk + gather.group) % 3 for q in range(3)] for p in range(3)]
        def add(p, a, c):
            return ((c - net.pos[a] + 4) % 4) * 4 ** own[p].index(a)

        xs = [[add(p, 0, x) + kk * 64 for x in range(4)] for p in range(3)]
        zs = [[add(p, 2, z) for z in range(4)] for p in range(3)]

        def body(y, _, kk=kk, xs=xs, zs=zs, add=add):
            ys = [add(p, 1, y) for p in range(3)]
            for z in range(4):
                yz = [ys[p] + zs[p][z] for p in range(3)]
                col = y * 2 + z // 2
                for x in range(4):
                    src = [yz[p] + xs[p][x] for p in range(3)]
                    tile = [gather.bufs[p][src[p], g] for p, g in GRANULE]
                    for t in range(2):
                        re = jnp.concatenate([tile[2 * t], tile[2 * t + 1]], 0)
                        im = jnp.concatenate([tile[4 + 2 * t], tile[5 + 2 * t]], 0)
                        first = row_base + (kk * 8 + (z % 2) * 4 + x) * 32 + t * 16
                        put(mats, lambda i: (i, col, pl.ds(first, 16)), re, im)
            return 0

        lax.fori_loop(0, 4, body, 0)


def product(mats, rows, z, base):
    dot = functools.partial(jnp.dot, preferred_element_type=F32)
    out = []
    for i in range(3):
        a_hi, a_lo = (jnp.concatenate([mats[2 * i + n, c, rows, :] for c in range(8)], 1) for n in range(2))
        z_hi, z_lo = z[base + 2 * i], z[base + 2 * i + 1]
        out.append(dot(a_hi, z_hi) + (dot(a_hi, z_lo) + dot(a_lo, z_hi)))
    return out[0] - out[1], out[2] - out[0] - out[1]


def wide(x):
    return jnp.concatenate([x, x], 1)


def kernel(frf, mount, recv_rows, codes, stiffness, loss, load, out, frf_v, *refs):
    h0, h1, rb = refs[0:3], refs[3:6], refs[6:9]
    amat, z, delta, load_c, y1_c, picked, sum1, got1, got2, got3, y1_own, y1_part, y1_sum, y1_all = refs[9:23]
    send, recv, misc_send, misc_recv, local = refs[23:]
    net = Net()
    k = net.k
    whole = pltpu.make_async_copy(frf, frf_v, local)
    whole.start()
    net.greet()
    lane = lax.broadcasted_iota(jnp.int32, (8, 128), 1)
    sub = lax.broadcasted_iota(jnp.int32, (8, 128), 0)

    gathers = [Gather(i, bufs, send, recv, net, picked) for i, bufs in enumerate((h0, h1, rb))]
    whole.wait()

    first_row = net.r * 4096
    cols = pl.ds(pl.multiple_of(net.v * 128, 128), 128)
    l_re = jnp.broadcast_to(load[0:1, cols], (8, 128))
    l_im = jnp.broadcast_to(load[1:2, cols], (8, 128))
    part = jnp.zeros((8, 128), F32)
    for t in range(8):
        at = [jnp.clip(mount[s % 4, net.r * 16 + t * 2 + s // 4] - first_row, 0, 4095) for s in range(8)]
        re, im = (jnp.concatenate([frf_v[c, pl.ds(i, 1), :] for i in at], 0) for c in range(2))
        for c, x in ((0, re), (1, im)):
            p, g = GRANULE[c * 4 + t % 4]
            (h0, h1)[t // 4][p][k * 64, g] = x
        y_re = jnp.sum(re * l_re - im * l_im, axis=1, keepdims=True)
        y_im = jnp.sum(re * l_im + im * l_re, axis=1, keepdims=True)
        part = part + jnp.where(lane == sub + t * 8, y_re, 0.0) + jnp.where(lane == sub + 64 + t * 8, y_im, 0.0)
    y1_own[0] = part
    net.greeted()

    def spread(src, dst, i, devs):
        for n, dev in enumerate(devs):
            pltpu.make_async_remote_copy(
                src_ref=src.at[0], dst_ref=dst.at[n], send_sem=misc_send.at[i], recv_sem=misc_recv.at[i],
                device_id=dev, device_id_type=MESH).start()

    def settle(ref, i):
        pltpu.make_async_copy(ref, ref, misc_send.at[i]).wait()

    def arrive(ref, i):
        pltpu.make_async_copy(ref, ref, misc_recv.at[i]).wait()

    spread(y1_own, y1_part, 0, net.same_row)
    gathers[0].first()
    gathers[1].first()

    def pick(b, _):
        zl, x, kk = b // 8, (b // 2) % 4, b % 2
        to = (kk * 4 + x) * 2 + zl
        for t in range(4):
            at = [recv_rows[b * 32 + t * 8 + s] - first_row for s in range(8)]
            inside = [(i >= 0) & (i < 4096) for i in at]
            at = [jnp.clip(i, 0, 4095) for i in at]
            for c in range(2):
                x8 = [jnp.where(inside[s], frf_v[c, pl.ds(at[s], 1), :], 0.0) for s in range(8)]
                picked[to, c * 4 + t] = jnp.concatenate(x8, 0)
        return 0

    lax.fori_loop(0, 16, pick, 0)
    mine, other = pl.ds(k * 8, 8), pl.ds((1 - k) * 8, 8)
    pltpu.make_async_remote_copy(
        src_ref=picked.at[other], dst_ref=got1, send_sem=misc_send.at[2], recv_sem=misc_recv.at[2],
        device_id=net.sib, device_id_type=MESH).start()

    code_b = codes[...].astype(F32).astype(BF16)
    for b in range(4):
        mount_of = lax.broadcasted_iota(jnp.int32, (256, 256), 0) // 4 + b * 64
        rep = (mount_of == lax.broadcasted_iota(jnp.int32, (256, 256), 1)).astype(F32).astype(BF16)
        delta[0, pl.ds(b * 256, 256), :] = lax.dot_general(rep, code_b, (((1,), (1,)), ((), ())), preferred_element_type=F32)

    gathers[0].second()
    gathers[1].second()

    arrive(y1_part, 0)
    total = y1_own[0]
    for i in range(7):
        total = total + y1_part[i]
    y1_sum[0] = total
    spread(y1_sum, y1_all, 1, net.same_var)

    arrive(got1, 2)
    sum1[...] = picked[mine] + got1[...]
    xx = net.pos[0]
    for n, d in enumerate((1, 2, 3)):
        pltpu.make_async_remote_copy(
            src_ref=sum1.at[pl.ds(((xx + d) % 4) * 2, 2)], dst_ref=got2.at[pl.ds(n * 2, 2)],
            send_sem=misc_send.at[3], recv_sem=misc_recv.at[3], device_id=net.near[0, d], device_id_type=MESH).start()

    for d in ORDER:
        gathers[0].third(d)
    for d in ORDER:
        gathers[1].third(d)

    for b in range(8):
        at = pl.ds(b * 128, 128)
        for c in range(2):
            load_c[c, at, :] = jnp.broadcast_to(load[c : c + 1, at], (128, 128)).T

    def table(ref):
        quarter = lax.broadcasted_iota(jnp.int32, (8, 256), 0) % 4
        out = []
        for l in range(LEVELS):
            x = jnp.where(quarter == 0, ref[0, l], ref[1, l])
            out.append(jnp.where(quarter == 2, ref[2, l], jnp.where(quarter == 3, ref[3, l], x)))
        return out

    stiff_t, loss_t = table(stiffness), table(loss)

    def look(j, _):
        rows = pl.ds(pl.multiple_of(j * 8, 8), 8)
        code = delta[0, rows, :]
        s, e = stiff_t[0], loss_t[0]
        for l in range(1, LEVELS):
            here = code == float(l)
            s, e = jnp.where(here, stiff_t[l], s), jnp.where(here, loss_t[l], e)
        delta[0, rows, :] = s
        delta[1, rows, :] = s * e
        return 0

    lax.fori_loop(0, 128, look, 0, unroll=4)

    def step(rows, y_re, y_im, to):
        d_re, d_im = delta[0, rows, :], delta[1, rows, :]
        z_re = wide(load_c[0, rows, :]) - (d_re * y_re - d_im * y_im)
        z_im = wide(load_c[1, rows, :]) - (d_re * y_im + d_im * y_re)
        put(z, lambda i: (to + i, rows), z_re, z_im)

    gathers[0].lasts(0)

    gathers[0].lasts(3)

    arrive(y1_all, 1)
    y1_c[pl.ds(net.r * 8, 8), :] = y1_sum[0]
    for i in range(15):
        y1_c[pl.ds(((net.r + 15 - i) % 16) * 8, 8), :] = y1_all[i]

    def begin(j, _):
        tile = y1_c[pl.ds(pl.multiple_of(j * 8, 8), 8), :]
        both = jnp.broadcast_to(jnp.sum(tile, axis=0, keepdims=True), (128, 128)).T
        for i in range(2):
            step(pl.ds(pl.multiple_of(j * 64 + i * 32, 32), 32), wide(both[i * 32 : i * 32 + 32]), wide(both[64 + i * 32 : 96 + i * 32]), 0)
        return 0

    lax.fori_loop(0, 16, begin, 0)

    arrive(got2, 3)
    sums = [sum1[xx * 2 + i] + got2[i] + got2[2 + i] + got2[4 + i] for i in range(2)]
    for i in range(2):
        got1[i] = sums[i]
    pltpu.make_async_remote_copy(
        src_ref=got1.at[1 - net.zl], dst_ref=got3, send_sem=misc_send.at[4], recv_sem=misc_recv.at[4],
        device_id=net.pair, device_id_type=MESH).start()

    gathers[0].lasts(1, 2)

    gathers[1].lasts(0)
    arrive(got3, 4)
    share = got1[net.zl] + got3[...]
    for i, (p, g) in enumerate(GRANULE):
        rb[p][k * 64, g] = share[i]
    gathers[2].first()
    gathers[0].cores()
    split(net, gathers[0], amat, 0)
    gathers[1].lasts(3, 1)

    def unit(u, _):
        @pl.when(u == 1)
        def _():
            gathers[1].lasts(2)
            gathers[2].second()
            gathers[1].cores()
            split(net, gathers[1], amat, 512)
            for d in ORDER:
                gathers[2].third(d)

        @pl.when(u == 4)
        def _():
            gathers[2].lasts(0, 3, 1, 2)

        @pl.when(u == 2 * ITERS - 2)
        def _():
            gathers[2].cores()
            split(net, gathers[2], amat, 1024)

        h, frm = u % 2, ((u // 2) % 2) * 6
        first = jnp.where(u == 2 * ITERS - 2, 1024, h * 512)
        y_re, y_im = product(amat, pl.ds(pl.multiple_of(first, 512), 512), z, frm)
        for j in range(16):
            here = slice(j * 32, j * 32 + 32)
            kk, zl, x = j // 8, (j // 4) % 2, j % 4
            to = (zl * 8 + x * 2 + kk) * 32
            out[0, pl.ds(to, 32), :] = y_re[here]
            out[1, pl.ds(to, 32), :] = y_im[here]
            step(pl.ds(pl.multiple_of(to * 2 + h * 32, 32), 32), y_re[here], y_im[here], 6 - frm)
        return 0

    lax.fori_loop(0, 2 * ITERS - 1, unit, 0)

    settle(y1_part, 0)
    settle(y1_all, 1)
    settle(got1, 2)
    settle(got2, 3)
    settle(got3, 4)
    for g in gathers:
        g.end(frf_v)


def on_device(frf, mount_rows, recv_rows, codes, stiffness, loss, load):
    vmem, smem = pl.BlockSpec(memory_space=pltpu.VMEM), pl.BlockSpec(memory_space=pltpu.SMEM)
    count = codes.shape[0]
    tile = (8, 128)
    found = pl.pallas_call(
        kernel,
        out_shape=jax.ShapeDtypeStruct((2, recv_rows.shape[0], count), F32),
        in_specs=[pl.BlockSpec(memory_space=pl.ANY), smem, smem, vmem, smem, smem, vmem],
        out_specs=vmem,
        scratch_shapes=[pltpu.VMEM(frf.shape, F32)]
        + [pltpu.VMEM((128, n) + tile, F32) for n in PART * 3]
        + [
            pltpu.VMEM((6, 8, 1536, 128), BF16),
            pltpu.VMEM((12, 1024, count), BF16),
            pltpu.VMEM((2, 1024, count), F32),
            pltpu.VMEM((2, 1024, 128), F32),
            pltpu.VMEM((128, 128), F32),
            pltpu.VMEM((16, 8) + tile, F32),
            pltpu.VMEM((8, 8) + tile, F32),
            pltpu.VMEM((8, 8) + tile, F32),
            pltpu.VMEM((6, 8) + tile, F32),
            pltpu.VMEM((8,) + tile, F32),
            pltpu.VMEM((1,) + tile, F32),
            pltpu.VMEM((7,) + tile, F32),
            pltpu.VMEM((1,) + tile, F32),
            pltpu.VMEM((15,) + tile, F32),
            pltpu.SemaphoreType.DMA((3,)),
            pltpu.SemaphoreType.DMA((3 * NREC,)),
            pltpu.SemaphoreType.DMA((5,)),
            pltpu.SemaphoreType.DMA((5,)),
            pltpu.SemaphoreType.DMA,
        ],
        compiler_params=pltpu.CompilerParams(collective_id=0, has_side_effects=True, vmem_limit_bytes=58 * 2**20),
        cost_estimate=pl.CostEstimate(flops=int(1.7e10), bytes_accessed=2**23, transcendentals=0),
    )(frf, mount_rows.T, recv_rows, codes, stiffness.T, loss.T, load)
    return jnp.swapaxes(found, 1, 2)


def solution(mesh):
    placed = (P(None, "row", "var"), P(), P(), P(("var", "row"), None), P(), P(), P())
    return jax.shard_map(
        on_device,
        mesh=mesh,
        in_specs=placed,
        out_specs=P(None, ("var", "row"), None),
        check_vma=False,
    )
```

```python
import functools

import jax
import jax.numpy as jnp
from jax import lax
from jax.experimental import pallas as pl
from jax.experimental.pallas import tpu as pltpu
from jax.sharding import PartitionSpec as P

MESH = pl.DeviceIdType.MESH
F32, BF16 = jnp.float32, jnp.bfloat16
ITERS = 4
LEVELS = 8
GRANULE = ((0, 0), (0, 1), (0, 2), (1, 0), (1, 1), (1, 2), (2, 0), (2, 1))
PART = (3, 3, 2)
ORDER = (1, 3, 2)
NREC = 20


def device(x, y, z, k):
    return {"var": y * 2 + z // 2, "row": (z % 2) * 8 + x * 2 + k}


class Net:
    def __init__(self):
        v, r = lax.axis_index("var"), lax.axis_index("row")
        y, zh = v // 2, v % 2
        zl, x, k = r // 8, (r // 2) % 4, r % 2
        z = zh * 2 + zl
        self.v, self.r, self.zl, self.zh, self.k = v, r, zl, zh, k
        self.pos = (x, y, z)
        self.near = {}
        for a in range(3):
            for d in (1, 2, 3):
                c = [x, y, z]
                c[a] = (c[a] + d) % 4
                self.near[a, d] = device(*c, k)
        self.sib = device(x, y, z, 1 - k)
        self.pair = {"var": v, "row": (1 - zl) * 8 + x * 2 + k}
        self.same_row = [{"var": (v + i) % 8, "row": r} for i in range(1, 8)]
        self.same_var = [{"var": v, "row": (r + i) % 16} for i in range(1, 16)]

    def along(self, turn, d):
        m, n = self.near[turn % 3, d], self.near[(turn + 1) % 3, d]
        return {q: jnp.where(self.k == 0, m[q], n[q]) for q in ("var", "row")}

    def greet(self):
        sem = pltpu.get_barrier_semaphore()
        for d in list(self.near.values()) + self.same_row + self.same_var:
            pl.semaphore_signal(sem, inc=1, device_id=d, device_id_type=MESH)

    def greeted(self):
        pl.semaphore_wait(pltpu.get_barrier_semaphore(), 9 + 7 + 15)


def slot(k, d3, d2, d1=0, n=1):
    return pl.ds(((k * 4 + d3) * 4 + d2) * 4 + d1, n)


class Gather:
    def __init__(self, group, bufs, send, recv, net, size_ref):
        self.group, self.bufs, self.net, self.size_ref = group, bufs, net, size_ref
        self.send, self.recv = send.at[group], recv
        self.count = 0

    def sem(self, kind, i=0):
        return self.recv.at[self.group * NREC + {"a": 0, "b": 0, "c": 4, "s": 16}[kind] + i]

    def go(self, p, src, dst, sem, dev):
        pltpu.make_async_remote_copy(
            src_ref=self.bufs[p].at[src], dst_ref=self.bufs[p].at[dst], send_sem=self.send, recv_sem=sem,
            device_id=dev, device_id_type=MESH).start()

    def wait(self, n, sem):
        ref = self.size_ref.at[pl.ds(0, n)]
        pltpu.make_async_copy(ref, ref, sem).wait()

    def dev(self, p, axis, d):
        return self.net.along(p + axis - 1 + self.group, d)

    def first(self):
        k = self.net.k
        for p in range(3):
            for d in ORDER:
                self.go(p, slot(k, 0, 0), slot(k, 0, 0, 4 - d), self.sem("a"), self.dev(p, 1, d))
        for p in range(3):
            self.send_b(p, (0, 1))
        for p in range(3):
            self.send_c(p, 0, (0, 1))

    def send_b(self, p, what):
        k = self.net.k
        for d in ORDER:
            self.go(p, slot(k, 0, 0, *what), slot(k, 0, 4 - d, *what), self.sem("b", d), self.dev(p, 2, d))

    def send_c(self, p, d2, what):
        k = self.net.k
        for d in ORDER:
            self.go(p, slot(k, 0, d2, *what), slot(k, 4 - d, d2, *what), self.sem("c", d2 * 3 + d - 1), self.dev(p, 3, d))

    def core(self, d3, d2):
        at = slot(self.net.k, d3, d2, 0, 4)
        for p in range(3):
            self.go(p, at, at, self.sem("s", d3), self.net.sib)

    def second(self):
        self.wait(3, self.sem("a"))
        for p in range(3):
            self.send_b(p, (1, 3))
        for p in range(3):
            self.send_c(p, 0, (1, 3))
        self.core(0, 0)

    def third(self, d):
        self.wait(4, self.sem("b", d))
        for p in range(3):
            self.send_c(p, 4 - d, (0, 4))
        self.core(0, 4 - d)

    def last(self, d2, d):
        self.wait(4, self.sem("c", d2 * 3 + d - 1))
        self.core(4 - d, d2)

    def lasts(self, *lines):
        for d2 in lines:
            for d in ORDER:
                self.last(d2, d)

    def cores(self):
        for d3 in range(4):
            self.wait(16, self.sem("s", d3))

    def end(self, frf_v):
        ref = frf_v.at[:, pl.ds(0, 127 * 32), :]
        pltpu.make_async_copy(ref, ref, self.send).wait()


def halves(x):
    hi = x.astype(BF16)
    return hi, (x - hi.astype(F32)).astype(BF16)


def put(ref, at, re, im):
    for i, x in enumerate((re, im, re + im)):
        hi, lo = halves(x)
        ref[at(2 * i)] = hi
        ref[at(2 * i + 1)] = lo


def split(net, gather, mats, row_base, cores=(0, 1)):
    for kk in cores:
        own = [[(p + q + kk + gather.group) % 3 for q in range(3)] for p in range(3)]
        def add(p, a, c):
            return ((c - net.pos[a] + 4) % 4) * 4 ** own[p].index(a)

        xs = [[add(p, 0, x) + kk * 64 for x in range(4)] for p in range(3)]
        zs = [[add(p, 2, z) for z in range(4)] for p in range(3)]

        def body(y, _, kk=kk, xs=xs, zs=zs, add=add):
            ys = [add(p, 1, y) for p in range(3)]
            for z in range(4):
                yz = [ys[p] + zs[p][z] for p in range(3)]
                col = y * 2 + z // 2
                for x in range(4):
                    src = [yz[p] + xs[p][x] for p in range(3)]
                    tile = [gather.bufs[p][src[p], g] for p, g in GRANULE]
                    for t in range(2):
                        re = jnp.concatenate([tile[2 * t], tile[2 * t + 1]], 0)
                        im = jnp.concatenate([tile[4 + 2 * t], tile[5 + 2 * t]], 0)
                        first = row_base + (kk * 8 + (z % 2) * 4 + x) * 32 + t * 16
                        put(mats, lambda i: (i, col, pl.ds(first, 16)), re, im)
            return 0

        lax.fori_loop(0, 4, body, 0)


def product(mats, rows, z, base):
    dot = functools.partial(jnp.dot, preferred_element_type=F32)
    out = []
    for i in range(3):
        a_hi, a_lo = (jnp.concatenate([mats[2 * i + n, c, rows, :] for c in range(8)], 1) for n in range(2))
        z_hi, z_lo = z[base + 2 * i], z[base + 2 * i + 1]
        out.append(dot(a_hi, z_hi) + (dot(a_hi, z_lo) + dot(a_lo, z_hi)))
    return out[0] - out[1], out[2] - out[0] - out[1]


def wide(x):
    return jnp.concatenate([x, x], 1)


def kernel(frf, mount, recv_rows, codes, stiffness, loss, load, out, frf_v, *refs):
    h0, h1, rb = refs[0:3], refs[3:6], refs[6:9]
    amat, z, delta, load_c, y1_c, picked, sum1, got1, got2, got3, y1_own, y1_part, y1_sum, y1_all = refs[9:23]
    send, recv, misc_send, misc_recv, local = refs[23:]
    net = Net()
    k = net.k
    whole = pltpu.make_async_copy(frf, frf_v, local)
    whole.start()
    net.greet()
    lane = lax.broadcasted_iota(jnp.int32, (8, 128), 1)
    sub = lax.broadcasted_iota(jnp.int32, (8, 128), 0)

    gathers = [Gather(i, bufs, send, recv, net, picked) for i, bufs in enumerate((h0, h1, rb))]
    whole.wait()

    first_row = net.r * 4096
    cols = pl.ds(pl.multiple_of(net.v * 128, 128), 128)
    l_re = jnp.broadcast_to(load[0:1, cols], (8, 128))
    l_im = jnp.broadcast_to(load[1:2, cols], (8, 128))
    part = jnp.zeros((8, 128), F32)
    for t in range(8):
        at = [jnp.clip(mount[s % 4, net.r * 16 + t * 2 + s // 4] - first_row, 0, 4095) for s in range(8)]
        re, im = (jnp.concatenate([frf_v[c, pl.ds(i, 1), :] for i in at], 0) for c in range(2))
        for c, x in ((0, re), (1, im)):
            p, g = GRANULE[c * 4 + t % 4]
            (h0, h1)[t // 4][p][k * 64, g] = x
        y_re = jnp.sum(re * l_re - im * l_im, axis=1, keepdims=True)
        y_im = jnp.sum(re * l_im + im * l_re, axis=1, keepdims=True)
        part = part + jnp.where(lane == sub + t * 8, y_re, 0.0) + jnp.where(lane == sub + 64 + t * 8, y_im, 0.0)
    y1_own[0] = part
    net.greeted()

    def spread(src, dst, i, devs):
        for n, dev in enumerate(devs):
            pltpu.make_async_remote_copy(
                src_ref=src.at[0], dst_ref=dst.at[n], send_sem=misc_send.at[i], recv_sem=misc_recv.at[i],
                device_id=dev, device_id_type=MESH).start()

    def settle(ref, i):
        pltpu.make_async_copy(ref, ref, misc_send.at[i]).wait()

    def arrive(ref, i):
        pltpu.make_async_copy(ref, ref, misc_recv.at[i]).wait()

    spread(y1_own, y1_part, 0, net.same_row)
    gathers[0].first()
    gathers[1].first()

    def pick(b, _):
        zl, x, kk = b // 8, (b // 2) % 4, b % 2
        to = (kk * 4 + x) * 2 + zl
        for t in range(4):
            at = [recv_rows[b * 32 + t * 8 + s] - first_row for s in range(8)]
            inside = [(i >= 0) & (i < 4096) for i in at]
            at = [jnp.clip(i, 0, 4095) for i in at]
            for c in range(2):
                x8 = [jnp.where(inside[s], frf_v[c, pl.ds(at[s], 1), :], 0.0) for s in range(8)]
                picked[to, c * 4 + t] = jnp.concatenate(x8, 0)
        return 0

    lax.fori_loop(0, 16, pick, 0)
    mine, other = pl.ds(k * 8, 8), pl.ds((1 - k) * 8, 8)
    pltpu.make_async_remote_copy(
        src_ref=picked.at[other], dst_ref=got1, send_sem=misc_send.at[2], recv_sem=misc_recv.at[2],
        device_id=net.sib, device_id_type=MESH).start()

    code_b = codes[...].astype(F32).astype(BF16)
    for b in range(4):
        mount_of = lax.broadcasted_iota(jnp.int32, (256, 256), 0) // 4 + b * 64
        rep = (mount_of == lax.broadcasted_iota(jnp.int32, (256, 256), 1)).astype(F32).astype(BF16)
        delta[0, pl.ds(b * 256, 256), :] = lax.dot_general(rep, code_b, (((1,), (1,)), ((), ())), preferred_element_type=F32)

    gathers[0].second()
    gathers[1].second()

    arrive(y1_part, 0)
    total = y1_own[0]
    for i in range(7):
        total = total + y1_part[i]
    y1_sum[0] = total
    spread(y1_sum, y1_all, 1, net.same_var)

    arrive(got1, 2)
    sum1[...] = picked[mine] + got1[...]
    xx = net.pos[0]
    for n, d in enumerate((1, 2, 3)):
        pltpu.make_async_remote_copy(
            src_ref=sum1.at[pl.ds(((xx + d) % 4) * 2, 2)], dst_ref=got2.at[pl.ds(n * 2, 2)],
            send_sem=misc_send.at[3], recv_sem=misc_recv.at[3], device_id=net.near[0, d], device_id_type=MESH).start()

    for d in ORDER:
        gathers[0].third(d)
    for d in ORDER:
        gathers[1].third(d)

    for b in range(8):
        at = pl.ds(b * 128, 128)
        for c in range(2):
            load_c[c, at, :] = jnp.broadcast_to(load[c : c + 1, at], (128, 128)).T

    def table(ref):
        quarter = lax.broadcasted_iota(jnp.int32, (8, 256), 0) % 4
        out = []
        for l in range(LEVELS):
            x = jnp.where(quarter == 0, ref[0, l], ref[1, l])
            out.append(jnp.where(quarter == 2, ref[2, l], jnp.where(quarter == 3, ref[3, l], x)))
        return out

    stiff_t, loss_t = table(stiffness), table(loss)

    def look(j, _):
        rows = pl.ds(pl.multiple_of(j * 8, 8), 8)
        code = delta[0, rows, :]
        s, e = stiff_t[0], loss_t[0]
        for l in range(1, LEVELS):
            here = code == float(l)
            s, e = jnp.where(here, stiff_t[l], s), jnp.where(here, loss_t[l], e)
        delta[0, rows, :] = s
        delta[1, rows, :] = s * e
        return 0

    lax.fori_loop(0, 128, look, 0, unroll=4)

    def step(rows, y_re, y_im, to):
        d_re, d_im = delta[0, rows, :], delta[1, rows, :]
        z_re = wide(load_c[0, rows, :]) - (d_re * y_re - d_im * y_im)
        z_im = wide(load_c[1, rows, :]) - (d_re * y_im + d_im * y_re)
        put(z, lambda i: (to + i, rows), z_re, z_im)

    gathers[0].lasts(0)

    gathers[0].lasts(3)

    arrive(y1_all, 1)
    y1_c[pl.ds(net.r * 8, 8), :] = y1_sum[0]
    for i in range(15):
        y1_c[pl.ds(((net.r + 15 - i) % 16) * 8, 8), :] = y1_all[i]

    def begin(j, _):
        tile = y1_c[pl.ds(pl.multiple_of(j * 8, 8), 8), :]
        both = jnp.broadcast_to(jnp.sum(tile, axis=0, keepdims=True), (128, 128)).T
        for i in range(2):
            step(pl.ds(pl.multiple_of(j * 64 + i * 32, 32), 32), wide(both[i * 32 : i * 32 + 32]), wide(both[64 + i * 32 : 96 + i * 32]), 0)
        return 0

    lax.fori_loop(0, 16, begin, 0)

    arrive(got2, 3)
    sums = [sum1[xx * 2 + i] + got2[i] + got2[2 + i] + got2[4 + i] for i in range(2)]
    for i in range(2):
        got1[i] = sums[i]
    pltpu.make_async_remote_copy(
        src_ref=got1.at[1 - net.zl], dst_ref=got3, send_sem=misc_send.at[4], recv_sem=misc_recv.at[4],
        device_id=net.pair, device_id_type=MESH).start()

    gathers[0].lasts(1, 2)

    gathers[1].lasts(0)
    arrive(got3, 4)
    share = got1[net.zl] + got3[...]
    for i, (p, g) in enumerate(GRANULE):
        rb[p][k * 64, g] = share[i]
    gathers[2].first()
    gathers[0].cores()
    split(net, gathers[0], amat, 0)
    gathers[1].lasts(3, 1)

    def unit(u, _):
        @pl.when(u == 1)
        def _():
            gathers[1].lasts(2)
            gathers[2].second()
            gathers[1].cores()
            split(net, gathers[1], amat, 512)

        @pl.when(u == 2)
        def _():
            for d in ORDER:
                gathers[2].third(d)

        @pl.when(u == 4)
        def _():
            gathers[2].lasts(0, 3)

        @pl.when(u == 5)
        def _():
            gathers[2].lasts(1, 2)

        @pl.when(u == 2 * ITERS - 2)
        def _():
            gathers[2].cores()
            split(net, gathers[2], amat, 1024)

        h, frm = u % 2, ((u // 2) % 2) * 6
        first = jnp.where(u == 2 * ITERS - 2, 1024, h * 512)
        y_re, y_im = product(amat, pl.ds(pl.multiple_of(first, 512), 512), z, frm)
        for j in range(16):
            here = slice(j * 32, j * 32 + 32)
            kk, zl, x = j // 8, (j // 4) % 2, j % 4
            to = (zl * 8 + x * 2 + kk) * 32
            out[0, pl.ds(to, 32), :] = y_re[here]
            out[1, pl.ds(to, 32), :] = y_im[here]
            step(pl.ds(pl.multiple_of(to * 2 + h * 32, 32), 32), y_re[here], y_im[here], 6 - frm)
        return 0

    lax.fori_loop(0, 2 * ITERS - 1, unit, 0)

    settle(y1_part, 0)
    settle(y1_all, 1)
    settle(got1, 2)
    settle(got2, 3)
    settle(got3, 4)
    for g in gathers:
        g.end(frf_v)


def on_device(frf, mount_rows, recv_rows, codes, stiffness, loss, load):
    vmem, smem = pl.BlockSpec(memory_space=pltpu.VMEM), pl.BlockSpec(memory_space=pltpu.SMEM)
    count = codes.shape[0]
    tile = (8, 128)
    found = pl.pallas_call(
        kernel,
        out_shape=jax.ShapeDtypeStruct((2, recv_rows.shape[0], count), F32),
        in_specs=[pl.BlockSpec(memory_space=pl.ANY), smem, smem, vmem, smem, smem, vmem],
        out_specs=vmem,
        scratch_shapes=[pltpu.VMEM(frf.shape, F32)]
        + [pltpu.VMEM((128, n) + tile, F32) for n in PART * 3]
        + [
            pltpu.VMEM((6, 8, 1536, 128), BF16),
            pltpu.VMEM((12, 1024, count), BF16),
            pltpu.VMEM((2, 1024, count), F32),
            pltpu.VMEM((2, 1024, 128), F32),
            pltpu.VMEM((128, 128), F32),
            pltpu.VMEM((16, 8) + tile, F32),
            pltpu.VMEM((8, 8) + tile, F32),
            pltpu.VMEM((8, 8) + tile, F32),
            pltpu.VMEM((6, 8) + tile, F32),
            pltpu.VMEM((8,) + tile, F32),
            pltpu.VMEM((1,) + tile, F32),
            pltpu.VMEM((7,) + tile, F32),
            pltpu.VMEM((1,) + tile, F32),
            pltpu.VMEM((15,) + tile, F32),
            pltpu.SemaphoreType.DMA((3,)),
            pltpu.SemaphoreType.DMA((3 * NREC,)),
            pltpu.SemaphoreType.DMA((5,)),
            pltpu.SemaphoreType.DMA((5,)),
            pltpu.SemaphoreType.DMA,
        ],
        compiler_params=pltpu.CompilerParams(collective_id=0, has_side_effects=True, vmem_limit_bytes=58 * 2**20),
        cost_estimate=pl.CostEstimate(flops=int(1.7e10), bytes_accessed=2**23, transcendentals=0),
    )(frf, mount_rows.T, recv_rows, codes, stiffness.T, loss.T, load)
    return jnp.swapaxes(found, 1, 2)


def solution(mesh):
    placed = (P(None, "row", "var"), P(), P(), P(("var", "row"), None), P(), P(), P())
    return jax.shard_map(
        on_device,
        mesh=mesh,
        in_specs=placed,
        out_specs=P(None, ("var", "row"), None),
        check_vma=False,
    )
```

```python
import functools

import jax
import jax.numpy as jnp
from jax import lax
from jax.experimental import pallas as pl
from jax.experimental.pallas import tpu as pltpu
from jax.sharding import PartitionSpec as P

MESH = pl.DeviceIdType.MESH
F32, BF16 = jnp.float32, jnp.bfloat16
ITERS = 4
LEVELS = 8
GRANULE = ((0, 0), (0, 1), (0, 2), (1, 0), (1, 1), (1, 2), (2, 0), (2, 1))
PART = (3, 3, 2)
ORDER = (1, 3, 2)
NREC = 20


def device(x, y, z, k):
    return {"var": y * 2 + z // 2, "row": (z % 2) * 8 + x * 2 + k}


class Net:
    def __init__(self):
        v, r = lax.axis_index("var"), lax.axis_index("row")
        y, zh = v // 2, v % 2
        zl, x, k = r // 8, (r // 2) % 4, r % 2
        z = zh * 2 + zl
        self.v, self.r, self.zl, self.zh, self.k = v, r, zl, zh, k
        self.pos = (x, y, z)
        self.near = {}
        for a in range(3):
            for d in (1, 2, 3):
                c = [x, y, z]
                c[a] = (c[a] + d) % 4
                self.near[a, d] = device(*c, k)
        self.sib = device(x, y, z, 1 - k)
        self.pair = {"var": v, "row": (1 - zl) * 8 + x * 2 + k}
        self.same_row = [{"var": (v + i) % 8, "row": r} for i in range(1, 8)]
        self.same_var = [{"var": v, "row": (r + i) % 16} for i in range(1, 16)]

    def along(self, turn, d):
        m, n = self.near[turn % 3, d], self.near[(turn + 1) % 3, d]
        return {q: jnp.where(self.k == 0, m[q], n[q]) for q in ("var", "row")}

    def greet(self):
        sem = pltpu.get_barrier_semaphore()
        for d in list(self.near.values()) + self.same_row + self.same_var:
            pl.semaphore_signal(sem, inc=1, device_id=d, device_id_type=MESH)

    def greeted(self):
        pl.semaphore_wait(pltpu.get_barrier_semaphore(), 9 + 7 + 15)


def slot(k, d3, d2, d1=0, n=1):
    return pl.ds(((k * 4 + d3) * 4 + d2) * 4 + d1, n)


class Gather:
    def __init__(self, group, bufs, send, recv, net, size_ref):
        self.group, self.bufs, self.net, self.size_ref = group, bufs, net, size_ref
        self.send, self.recv = send.at[group], recv
        self.count = 0

    def sem(self, kind, i=0):
        return self.recv.at[self.group * NREC + {"a": 0, "b": 0, "c": 4, "s": 16}[kind] + i]

    def go(self, p, src, dst, sem, dev):
        pltpu.make_async_remote_copy(
            src_ref=self.bufs[p].at[src], dst_ref=self.bufs[p].at[dst], send_sem=self.send, recv_sem=sem,
            device_id=dev, device_id_type=MESH).start()

    def wait(self, n, sem):
        ref = self.size_ref.at[pl.ds(0, n)]
        pltpu.make_async_copy(ref, ref, sem).wait()

    def dev(self, p, axis, d):
        return self.net.along(p + axis - 1 + self.group, d)

    def first(self):
        k = self.net.k
        for p in range(3):
            for d in ORDER:
                self.go(p, slot(k, 0, 0), slot(k, 0, 0, 4 - d), self.sem("a"), self.dev(p, 1, d))
        for p in range(3):
            self.send_b(p, (0, 1))
        for p in range(3):
            self.send_c(p, 0, (0, 1))

    def send_b(self, p, what):
        k = self.net.k
        for d in ORDER:
            self.go(p, slot(k, 0, 0, *what), slot(k, 0, 4 - d, *what), self.sem("b", d), self.dev(p, 2, d))

    def send_c(self, p, d2, what):
        k = self.net.k
        for d in ORDER:
            self.go(p, slot(k, 0, d2, *what), slot(k, 4 - d, d2, *what), self.sem("c", d2 * 3 + d - 1), self.dev(p, 3, d))

    def core(self, d3, d2):
        at = slot(self.net.k, d3, d2, 0, 4)
        for p in range(3):
            self.go(p, at, at, self.sem("s", d3), self.net.sib)

    def second(self):
        self.wait(3, self.sem("a"))
        for p in range(3):
            self.send_b(p, (1, 3))

    def second_c(self):
        for p in range(3):
            self.send_c(p, 0, (1, 3))
        self.core(0, 0)

    def third(self, d):
        self.wait(4, self.sem("b", d))
        for p in range(3):
            self.send_c(p, 4 - d, (0, 4))
        self.core(0, 4 - d)

    def last(self, d2, d):
        self.wait(4, self.sem("c", d2 * 3 + d - 1))
        self.core(4 - d, d2)

    def lasts(self, *lines):
        for d2 in lines:
            for d in ORDER:
                self.last(d2, d)

    def cores(self):
        for d3 in range(4):
            self.wait(16, self.sem("s", d3))

    def end(self, frf_v):
        ref = frf_v.at[:, pl.ds(0, 127 * 32), :]
        pltpu.make_async_copy(ref, ref, self.send).wait()


def halves(x):
    hi = x.astype(BF16)
    return hi, (x - hi.astype(F32)).astype(BF16)


def put(ref, at, re, im):
    for i, x in enumerate((re, im, re + im)):
        hi, lo = halves(x)
        ref[at(2 * i)] = hi
        ref[at(2 * i + 1)] = lo


def split(net, gather, mats, row_base, cores=(0, 1)):
    for kk in cores:
        own = [[(p + q + kk + gather.group) % 3 for q in range(3)] for p in range(3)]
        def add(p, a, c):
            return ((c - net.pos[a] + 4) % 4) * 4 ** own[p].index(a)

        xs = [[add(p, 0, x) + kk * 64 for x in range(4)] for p in range(3)]
        zs = [[add(p, 2, z) for z in range(4)] for p in range(3)]

        def body(y, _, kk=kk, xs=xs, zs=zs, add=add):
            ys = [add(p, 1, y) for p in range(3)]
            for z in range(4):
                yz = [ys[p] + zs[p][z] for p in range(3)]
                col = y * 2 + z // 2
                for x in range(4):
                    src = [yz[p] + xs[p][x] for p in range(3)]
                    tile = [gather.bufs[p][src[p], g] for p, g in GRANULE]
                    for t in range(2):
                        re = jnp.concatenate([tile[2 * t], tile[2 * t + 1]], 0)
                        im = jnp.concatenate([tile[4 + 2 * t], tile[5 + 2 * t]], 0)
                        first = row_base + (kk * 8 + (z % 2) * 4 + x) * 32 + t * 16
                        put(mats, lambda i: (i, col, pl.ds(first, 16)), re, im)
            return 0

        lax.fori_loop(0, 4, body, 0)


def product(mats, rows, z, base):
    dot = functools.partial(jnp.dot, preferred_element_type=F32)
    out = []
    for i in range(3):
        a_hi, a_lo = (jnp.concatenate([mats[2 * i + n, c, rows, :] for c in range(8)], 1) for n in range(2))
        z_hi, z_lo = z[base + 2 * i], z[base + 2 * i + 1]
        out.append(dot(a_hi, z_hi) + (dot(a_hi, z_lo) + dot(a_lo, z_hi)))
    return out[0] - out[1], out[2] - out[0] - out[1]


def wide(x):
    return jnp.concatenate([x, x], 1)


def kernel(frf, mount, recv_rows, codes, stiffness, loss, load, out, frf_v, *refs):
    h0, h1, rb = refs[0:3], refs[3:6], refs[6:9]
    amat, z, delta, load_c, y1_c, picked, sum1, got1, got2, got3, y1_own, y1_part, y1_sum, y1_all = refs[9:23]
    send, recv, misc_send, misc_recv, local = refs[23:]
    net = Net()
    k = net.k
    whole = pltpu.make_async_copy(frf, frf_v, local)
    whole.start()
    net.greet()
    lane = lax.broadcasted_iota(jnp.int32, (8, 128), 1)
    sub = lax.broadcasted_iota(jnp.int32, (8, 128), 0)

    gathers = [Gather(i, bufs, send, recv, net, picked) for i, bufs in enumerate((h0, h1, rb))]
    whole.wait()

    first_row = net.r * 4096
    cols = pl.ds(pl.multiple_of(net.v * 128, 128), 128)
    l_re = jnp.broadcast_to(load[0:1, cols], (8, 128))
    l_im = jnp.broadcast_to(load[1:2, cols], (8, 128))
    part = jnp.zeros((8, 128), F32)
    for t in range(8):
        at = [jnp.clip(mount[s % 4, net.r * 16 + t * 2 + s // 4] - first_row, 0, 4095) for s in range(8)]
        re, im = (jnp.concatenate([frf_v[c, pl.ds(i, 1), :] for i in at], 0) for c in range(2))
        for c, x in ((0, re), (1, im)):
            p, g = GRANULE[c * 4 + t % 4]
            (h0, h1)[t // 4][p][k * 64, g] = x
        y_re = jnp.sum(re * l_re - im * l_im, axis=1, keepdims=True)
        y_im = jnp.sum(re * l_im + im * l_re, axis=1, keepdims=True)
        part = part + jnp.where(lane == sub + t * 8, y_re, 0.0) + jnp.where(lane == sub + 64 + t * 8, y_im, 0.0)
    y1_own[0] = part
    net.greeted()

    def spread(src, dst, i, devs):
        for n, dev in enumerate(devs):
            pltpu.make_async_remote_copy(
                src_ref=src.at[0], dst_ref=dst.at[n], send_sem=misc_send.at[i], recv_sem=misc_recv.at[i],
                device_id=dev, device_id_type=MESH).start()

    def settle(ref, i):
        pltpu.make_async_copy(ref, ref, misc_send.at[i]).wait()

    def arrive(ref, i):
        pltpu.make_async_copy(ref, ref, misc_recv.at[i]).wait()

    spread(y1_own, y1_part, 0, net.same_row)
    gathers[0].first()
    gathers[1].first()

    def pick(b, _):
        zl, x, kk = b // 8, (b // 2) % 4, b % 2
        to = (kk * 4 + x) * 2 + zl
        for t in range(4):
            at = [recv_rows[b * 32 + t * 8 + s] - first_row for s in range(8)]
            inside = [(i >= 0) & (i < 4096) for i in at]
            at = [jnp.clip(i, 0, 4095) for i in at]
            for c in range(2):
                x8 = [jnp.where(inside[s], frf_v[c, pl.ds(at[s], 1), :], 0.0) for s in range(8)]
                picked[to, c * 4 + t] = jnp.concatenate(x8, 0)
        return 0

    lax.fori_loop(0, 16, pick, 0)
    mine, other = pl.ds(k * 8, 8), pl.ds((1 - k) * 8, 8)
    pltpu.make_async_remote_copy(
        src_ref=picked.at[other], dst_ref=got1, send_sem=misc_send.at[2], recv_sem=misc_recv.at[2],
        device_id=net.sib, device_id_type=MESH).start()

    code_b = codes[...].astype(F32).astype(BF16)
    for b in range(4):
        mount_of = lax.broadcasted_iota(jnp.int32, (256, 256), 0) // 4 + b * 64
        rep = (mount_of == lax.broadcasted_iota(jnp.int32, (256, 256), 1)).astype(F32).astype(BF16)
        delta[0, pl.ds(b * 256, 256), :] = lax.dot_general(rep, code_b, (((1,), (1,)), ((), ())), preferred_element_type=F32)

    gathers[0].second()
    gathers[1].second()
    gathers[0].second_c()
    gathers[1].second_c()

    arrive(y1_part, 0)
    total = y1_own[0]
    for i in range(7):
        total = total + y1_part[i]
    y1_sum[0] = total
    spread(y1_sum, y1_all, 1, net.same_var)

    arrive(got1, 2)
    sum1[...] = picked[mine] + got1[...]
    xx = net.pos[0]
    for n, d in enumerate((1, 2, 3)):
        pltpu.make_async_remote_copy(
            src_ref=sum1.at[pl.ds(((xx + d) % 4) * 2, 2)], dst_ref=got2.at[pl.ds(n * 2, 2)],
            send_sem=misc_send.at[3], recv_sem=misc_recv.at[3], device_id=net.near[0, d], device_id_type=MESH).start()

    for d in ORDER:
        gathers[0].third(d)
    for d in ORDER:
        gathers[1].third(d)

    for b in range(8):
        at = pl.ds(b * 128, 128)
        for c in range(2):
            load_c[c, at, :] = jnp.broadcast_to(load[c : c + 1, at], (128, 128)).T

    def table(ref):
        quarter = lax.broadcasted_iota(jnp.int32, (8, 256), 0) % 4
        out = []
        for l in range(LEVELS):
            x = jnp.where(quarter == 0, ref[0, l], ref[1, l])
            out.append(jnp.where(quarter == 2, ref[2, l], jnp.where(quarter == 3, ref[3, l], x)))
        return out

    stiff_t, loss_t = table(stiffness), table(loss)

    def look(j, _):
        rows = pl.ds(pl.multiple_of(j * 8, 8), 8)
        code = delta[0, rows, :]
        s, e = stiff_t[0], loss_t[0]
        for l in range(1, LEVELS):
            here = code == float(l)
            s, e = jnp.where(here, stiff_t[l], s), jnp.where(here, loss_t[l], e)
        delta[0, rows, :] = s
        delta[1, rows, :] = s * e
        return 0

    lax.fori_loop(0, 128, look, 0, unroll=4)

    def step(rows, y_re, y_im, to):
        d_re, d_im = delta[0, rows, :], delta[1, rows, :]
        z_re = wide(load_c[0, rows, :]) - (d_re * y_re - d_im * y_im)
        z_im = wide(load_c[1, rows, :]) - (d_re * y_im + d_im * y_re)
        put(z, lambda i: (to + i, rows), z_re, z_im)

    gathers[0].lasts(0)

    arrive(y1_all, 1)
    y1_c[pl.ds(net.r * 8, 8), :] = y1_sum[0]
    for i in range(15):
        y1_c[pl.ds(((net.r + 15 - i) % 16) * 8, 8), :] = y1_all[i]

    def begin(j, _):
        tile = y1_c[pl.ds(pl.multiple_of(j * 8, 8), 8), :]
        both = jnp.broadcast_to(jnp.sum(tile, axis=0, keepdims=True), (128, 128)).T
        for i in range(2):
            step(pl.ds(pl.multiple_of(j * 64 + i * 32, 32), 32), wide(both[i * 32 : i * 32 + 32]), wide(both[64 + i * 32 : 96 + i * 32]), 0)
        return 0

    lax.fori_loop(0, 16, begin, 0, unroll=2)

    arrive(got2, 3)
    sums = [sum1[xx * 2 + i] + got2[i] + got2[2 + i] + got2[4 + i] for i in range(2)]
    for i in range(2):
        got1[i] = sums[i]
    pltpu.make_async_remote_copy(
        src_ref=got1.at[1 - net.zl], dst_ref=got3, send_sem=misc_send.at[4], recv_sem=misc_recv.at[4],
        device_id=net.pair, device_id_type=MESH).start()

    gathers[0].lasts(3)
    gathers[0].lasts(1, 2)

    gathers[1].lasts(0)
    arrive(got3, 4)
    share = got1[net.zl] + got3[...]
    for i, (p, g) in enumerate(GRANULE):
        rb[p][k * 64, g] = share[i]
    gathers[2].first()
    gathers[0].cores()
    split(net, gathers[0], amat, 0)
    gathers[1].lasts(3, 1)

    def unit(u, _):
        @pl.when(u == 1)
        def _():
            gathers[1].lasts(2)
            gathers[2].second()
            gathers[2].second_c()
            gathers[1].cores()
            split(net, gathers[1], amat, 512)

        @pl.when(u == 2)
        def _():
            for d in ORDER:
                gathers[2].third(d)

        @pl.when(u == 4)
        def _():
            gathers[2].lasts(0, 3)

        @pl.when(u == 5)
        def _():
            gathers[2].lasts(1, 2)

        @pl.when(u == 2 * ITERS - 2)
        def _():
            gathers[2].cores()
            split(net, gathers[2], amat, 1024)

        h, frm = u % 2, ((u // 2) % 2) * 6
        first = jnp.where(u == 2 * ITERS - 2, 1024, h * 512)
        y_re, y_im = product(amat, pl.ds(pl.multiple_of(first, 512), 512), z, frm)
        for j in range(16):
            here = slice(j * 32, j * 32 + 32)
            kk, zl, x = j // 8, (j // 4) % 2, j % 4
            to = (zl * 8 + x * 2 + kk) * 32
            out[0, pl.ds(to, 32), :] = y_re[here]
            out[1, pl.ds(to, 32), :] = y_im[here]
            step(pl.ds(pl.multiple_of(to * 2 + h * 32, 32), 32), y_re[here], y_im[here], 6 - frm)
        return 0

    lax.fori_loop(0, 2 * ITERS - 1, unit, 0)

    settle(y1_part, 0)
    settle(y1_all, 1)
    settle(got1, 2)
    settle(got2, 3)
    settle(got3, 4)
    for g in gathers:
        g.end(frf_v)


def on_device(frf, mount_rows, recv_rows, codes, stiffness, loss, load):
    vmem, smem = pl.BlockSpec(memory_space=pltpu.VMEM), pl.BlockSpec(memory_space=pltpu.SMEM)
    count = codes.shape[0]
    tile = (8, 128)
    found = pl.pallas_call(
        kernel,
        out_shape=jax.ShapeDtypeStruct((2, recv_rows.shape[0], count), F32),
        in_specs=[pl.BlockSpec(memory_space=pl.ANY), smem, smem, vmem, smem, smem, vmem],
        out_specs=vmem,
        scratch_shapes=[pltpu.VMEM(frf.shape, F32)]
        + [pltpu.VMEM((128, n) + tile, F32) for n in PART * 3]
        + [
            pltpu.VMEM((6, 8, 1536, 128), BF16),
            pltpu.VMEM((12, 1024, count), BF16),
            pltpu.VMEM((2, 1024, count), F32),
            pltpu.VMEM((2, 1024, 128), F32),
            pltpu.VMEM((128, 128), F32),
            pltpu.VMEM((16, 8) + tile, F32),
            pltpu.VMEM((8, 8) + tile, F32),
            pltpu.VMEM((8, 8) + tile, F32),
            pltpu.VMEM((6, 8) + tile, F32),
            pltpu.VMEM((8,) + tile, F32),
            pltpu.VMEM((1,) + tile, F32),
            pltpu.VMEM((7,) + tile, F32),
            pltpu.VMEM((1,) + tile, F32),
            pltpu.VMEM((15,) + tile, F32),
            pltpu.SemaphoreType.DMA((3,)),
            pltpu.SemaphoreType.DMA((3 * NREC,)),
            pltpu.SemaphoreType.DMA((5,)),
            pltpu.SemaphoreType.DMA((5,)),
            pltpu.SemaphoreType.DMA,
        ],
        compiler_params=pltpu.CompilerParams(collective_id=0, has_side_effects=True, vmem_limit_bytes=58 * 2**20),
        cost_estimate=pl.CostEstimate(flops=int(1.7e10), bytes_accessed=2**23, transcendentals=0),
    )(frf, mount_rows.T, recv_rows, codes, stiffness.T, loss.T, load)
    return jnp.swapaxes(found, 1, 2)


def solution(mesh):
    placed = (P(None, "row", "var"), P(), P(), P(("var", "row"), None), P(), P(), P())
    return jax.shard_map(
        on_device,
        mesh=mesh,
        in_specs=placed,
        out_specs=P(None, ("var", "row"), None),
        check_vma=False,
    )
```
